512 devices in a mesh: wide: 64 (over y, x, core), narrow: 8 (over z).
Axes of the slice: x: 4, y: 8, z: 8, core: 2. Of those that a mesh axis runs over, the one named last changes fastest.
Arguments:
- right_side: float32 [512, 128, 256], P('wide', 'narrow'), may hold values from -8 to 8
- coefficient: float32 [512, 128, 256], P('wide', 'narrow'), may hold values from 0.2 to 5
Outputs:
- correction: float32 [512, 128, 256], P('wide', 'narrow')
The draws below stay inside these ranges and needn't reach their ends.
All inputs are finite; a program needn't handle non-finite values.
Results may differ from the reference program's by a relative error of at most 0.0001.
Values sent between devices are 32-bit elements; how exact they have to be, the bound alone decides.
A program may use at most 64 MiB of HBM per device.

```python
import math
import jax
import jax.numpy as jnp

NZ = 256
COARSE_ITERS = 5
NX = 512
NY = 128


def block_levels(own_key, shape, shards, smallest, high):
    def one(dim, blocks):
        steps = jax.random.uniform(jax.random.fold_in(jax.random.fold_in(own_key, 6), dim), (blocks,), jnp.float32, smallest / len(shards), high / len(shards))
        return jnp.repeat(jnp.exp(steps), shape[dim] // blocks).reshape((-1,) + (1,) * (len(shape) - dim - 1))

    factor_of = one(*shards[0])
    for cut in shards[1:]:
        factor_of = factor_of * one(*cut)
    return factor_of


def normal_values(key, dims, width, most, pieces=(), kind=jnp.bfloat16):
    factor_of = block_levels(key, dims, pieces, -0.22, 0.18) if pieces else 1.0
    array = jax.random.normal(key, dims, jnp.float32) * width * factor_of
    return jnp.minimum(jnp.maximum(array, -most), most).astype(kind)


def setup_inputs(seed: int = 0) -> dict:
    key_list = jax.random.split(jax.random.key(seed), 3)
    right_side = normal_values(key_list[0], (NX, NY, NZ), 1.0, 8.0, ((0, 64), (1, 8)), jnp.float32)
    coefficient = jnp.clip(jnp.exp(math.log(5.0) - 3.218876 * jax.random.uniform(key_list[1], (NX, NY, NZ), jnp.float32) ** block_levels(key_list[1], (NX, NY, NZ), ((0, 64), (1, 8)), -0.2, 0.2)), 0.2, 5.0)
    return {"right_side": right_side, "coefficient": coefficient}


OMEGA = 0.8


def pad_plane(x):
    return jnp.pad(x, ((1, 1), (1, 1), (0, 0)))


def neighbours(vx, kx):
    vz = jnp.pad(vx[1:-1, 1:-1], ((0, 0), (0, 0), (1, 1)))
    kz = jnp.pad(kx[1:-1, 1:-1], ((0, 0), (0, 0), (1, 1)))
    return [(vx[2:, 1:-1], kx[2:, 1:-1]), (vx[:-2, 1:-1], kx[:-2, 1:-1]),
            (vx[1:-1, 2:], kx[1:-1, 2:]), (vx[1:-1, :-2], kx[1:-1, :-2]),
            (vz[:, :, 2:], kz[:, :, 2:]), (vz[:, :, :-2], kz[:, :, :-2])]


def local_apply(vx, kx):
    center = vx[1:-1, 1:-1]
    kc = kx[1:-1, 1:-1]
    image = jnp.zeros_like(center)
    diag = jnp.zeros_like(center)
    for vn, kn in neighbours(vx, kx):
        face = 0.5 * (kc + kn)
        image = image + face * (center - vn)
        diag = diag + face
    return image, diag


def relax(ex, r, kx):
    image, diag = local_apply(ex, kx)
    return ex[1:-1, 1:-1] + OMEGA * (r - image) / diag


def restrict(x):
    a, b, c = x.shape
    return jnp.sum(x.reshape(a // 2, 2, b // 2, 2, c // 2, 2), axis=(1, 3, 5)) * 0.5


def coarsen(k):
    a, b, c = k.shape
    return jnp.sum(k.reshape(a // 2, 2, b // 2, 2, c // 2, 2), axis=(1, 3, 5)) * 0.125


def prolong(x):
    return jnp.repeat(jnp.repeat(jnp.repeat(x, 2, axis=0), 2, axis=1), 2, axis=2)


def descend(r, k):
    kx = pad_plane(k)
    diag = local_apply(jnp.zeros_like(kx), kx)[1]
    e = OMEGA * r / diag
    e = relax(pad_plane(e), r, kx)
    image = local_apply(pad_plane(e), kx)[0]
    return e, restrict(r - image)


def ascend(e, r, k):
    kx = pad_plane(k)
    e = relax(pad_plane(e), r, kx)
    e = relax(pad_plane(e), r, kx)
    return e


def coarse_solve(r, k):
    kx = pad_plane(k)
    solution = jnp.zeros_like(r)
    residual = r
    direction = r
    norm_now = jnp.sum(residual * residual)
    for step in range(COARSE_ITERS):
        image = local_apply(pad_plane(direction), kx)[0]
        alpha = norm_now / jnp.sum(direction * image)
        solution = solution + alpha * direction
        residual = residual - alpha * image
        norm_next = jnp.sum(residual * residual)
        direction = residual + (norm_next / norm_now) * direction
        norm_now = norm_next
    return solution


def reference(right_side, coefficient):
    k0 = coefficient
    e0, r1 = descend(right_side, k0)
    k1 = coarsen(k0)
    e1, r2 = descend(r1, k1)
    k2 = coarsen(k1)
    e2, r3 = descend(r2, k2)
    k3 = coarsen(k2)
    e3 = coarse_solve(r3, k3)
    e2 = ascend(e2 + prolong(e3), r2, k2)
    e1 = ascend(e1 + prolong(e2), r1, k1)
    e0 = ascend(e0 + prolong(e1), right_side, k0)
    return e0
```

```python
import functools

import jax
import jax.numpy as jnp
from jax import lax
from jax.experimental import pallas as pl
from jax.experimental.pallas import tpu as pltpu
from jax.sharding import PartitionSpec as P

COARSE_ITERS = 5
OMEGA = 0.8
MESH = pl.DeviceIdType.MESH
F32 = jnp.float32

OWN = 7
PLANES = 22
HALO_K, HALO_R = 7, 6
OWN1 = 3
PLANES1 = 10


def split(x):
    high = x.astype(jnp.bfloat16)
    rest = x - high.astype(F32)
    middle = rest.astype(jnp.bfloat16)
    low = (rest - middle.astype(F32)).astype(jnp.bfloat16)
    return high, middle, low


def times_right(x, zero_one):
    rows = x.shape[0]
    out = jnp.dot(jnp.concatenate(split(x), axis=0), zero_one, preferred_element_type=F32)
    return out[:rows] + out[rows : 2 * rows] + out[2 * rows :]


def times_left(zero_one, x):
    columns = x.shape[1]
    out = jnp.dot(zero_one, jnp.concatenate(split(x), axis=1), preferred_element_type=F32)
    return out[:, :columns] + out[:, columns : 2 * columns] + out[:, 2 * columns :]


def iotas(rows, columns):
    shape = (rows, columns)
    return lax.broadcasted_iota(jnp.int32, shape, 0), lax.broadcasted_iota(jnp.int32, shape, 1)


def zero_one(condition):
    return jnp.where(condition, 1.0, 0.0).astype(jnp.bfloat16)


def halve_z():
    fine, coarse = iotas(256, 128)
    return zero_one(fine // 2 == coarse)


def double_z():
    coarse, fine = iotas(128, 256)
    return zero_one(fine // 2 == coarse)


def weights(first, last, k, wx, wy, wz, diag, inv):
    rows, columns = k.shape[1:]
    lane = lax.broadcasted_iota(jnp.int32, (rows, columns), 1)
    rim = jnp.where((lane == 0) | (lane == columns - 1), 0.5, 0.0)
    half = jnp.where(lane == columns - 1, 0.0, 0.5)
    wx[first - 1] = 0.5 * (k[first - 1] + k[first])

    def plane(p):
        here = k[p]
        x = 0.5 * (here + k[p + 1])
        y = 0.5 * (here + pltpu.roll(here, rows - 1, 0))
        z = half * (here + pltpu.roll(here, columns - 1, 1))
        d = (x + wx[p - 1]) + (y + pltpu.roll(y, 1, 0)) + (z + pltpu.roll(z, 1, 1)) + rim * here
        wx[p] = x
        wy[p] = y
        wz[p] = z
        diag[p] = d
        inv[p] = jnp.where(here > 0.0, OMEGA / d, 0.0)

    return plane


def image_at(p, v, wx, wy, wz, diag):
    rows, columns = v.shape[1:]
    here = v[p]
    y, z = wy[p], wz[p]
    total = wx[p] * v[p + 1] + wx[p - 1] * v[p - 1]
    total += y * pltpu.roll(here, rows - 1, 0) + pltpu.roll(y * here, 1, 0)
    total += z * pltpu.roll(here, columns - 1, 1) + pltpu.roll(z * here, 1, 1)
    return diag[p] * here - total


def loop(first, last, body, unroll):
    if unroll:
        for p in range(first, last):
            body(p)
    else:

        def step(p, carry):
            body(p)
            return carry

        lax.fori_loop(first, last, step, 0)


def corner_pack(k, r, x_low, y_low):
    sub = lax.broadcasted_iota(jnp.int32, (8, 256), 0)
    near = 7 - sub if y_low else sub
    turn = lambda x, by: pltpu.roll(x, (by if y_low else -by) % 8, 0)
    return [
        jnp.where(near < 6, k(1), turn(k(5), 2)),
        jnp.where(near < 5, k(2), turn(r(3), 3)),
        jnp.where(near < 4, k(3), turn(r(2), 4)),
        jnp.where(near < 5, r(1), turn(k(4), 3)),
        jnp.where(near < 2, r(4), jnp.where(near == 2, turn(r(5), -2), turn(k(6), -3))),
    ]


def corner_unpack(tiles, y_low):
    turn = lambda x, by: pltpu.roll(x, (by if y_low else -by) % 8, 0)
    one, two, three, four, five = tiles
    k = [one, two, three, turn(four, -3), turn(one, -2), turn(five, 3)]
    r = [four, turn(three, -4), turn(two, -3), five, turn(five, 2)]
    return k, r


def kernel(nw, nn, r_in, k_in, out, *refs):
    (K0, R0, EA, EB, WX, WY, WZ, DG, IV, XS, CS, CR, T0,
     K1, R1, A1, B1, WX1, WY1, WZ1, DG1, IV1, E1S, E1G, T1,
     SB2, G2, KS, GK, K2X, K2S, K3S, K3G, R3S, R3G, F3,
     X3, Y3, Z3, D3, S3, Q3, P3, MB, E2G, E3, DS,
     load, halo_s, halo_r, kz_s, kz_r, rz_s, rz_r, kx_s, kx_r, e1_s, e1_r,
     k3_s, k3_r, r3_s, r3_r, e2_s, e2_r) = refs
    w, n = lax.axis_index("wide"), lax.axis_index("narrow")
    wide = lambda d: lax.rem(w + (d + nw), nw)
    narrow = lambda d: lax.rem(n + (d + nn), nn)

    def outside(dx, dy):
        over = jnp.int32(0)
        if dx:
            over = over + jnp.where(w == (nw - 1 if dx > 0 else 0), 1, 0)
            if abs(dx) == 2:
                over = over + jnp.where(w == (nw - 2 if dx > 0 else 1), 1, 0)
        if dy:
            over = over + jnp.where(n == (nn - 1 if dy > 0 else 0), 1, 0)
        return jnp.where(over > 0, 1, 0)

    def remote(src, dst, send, recv, to):
        return pltpu.make_async_remote_copy(
            src_ref=src, dst_ref=dst, send_sem=send, recv_sem=recv, device_id=to, device_id_type=MESH
        )

    load_k = pltpu.make_async_copy(k_in, K0.at[OWN : OWN + 8, 0:16], load.at[0])
    load_r = pltpu.make_async_copy(r_in, R0.at[OWN : OWN + 8, 0:16], load.at[1])
    load_k.start()
    load_r.start()
    barrier = pltpu.get_barrier_semaphore()

    def greet_wide(d, carry):
        pl.semaphore_signal(barrier, inc=1, device_id=(wide(d), n), device_id_type=MESH)
        return carry

    def greet_narrow(d, carry):
        for dx in (-1, 0, 1):
            pl.semaphore_signal(barrier, inc=1, device_id=(wide(dx), narrow(d)), device_id_type=MESH)
        return carry

    lax.fori_loop(1, nn, greet_narrow, 0)
    lax.fori_loop(1, nw, greet_wide, 0)

    zero_planes = jnp.zeros((8, 16, 256), F32)
    K0[PLANES : PLANES + 8, 0:16] = zero_planes
    R0[PLANES : PLANES + 8, 0:16] = zero_planes
    zero_rows = jnp.zeros((16, 256), F32)
    for p in (0, 21):
        K0[p, 16:32] = zero_rows
    for p in (1, 20):
        R0[p, 16:32] = zero_rows
    SB2[1] = jnp.zeros((4, 128), F32)
    K2X[1] = jnp.zeros((32, 128), F32)
    MB[1] = jnp.zeros((2, 32, 128), F32)
    E1S[1] = jnp.zeros((4, 3, 8, 128), F32)
    E3[...] = jnp.zeros((4, nw + 16, 128), F32)
    load_k.wait()
    load_r.wait()

    corners = [(dx, dy) for dx in (-1, 1) for dy in (-1, 1)]
    for i, (dx, dy) in enumerate(corners):
        rows = pl.ds(8, 8) if dy > 0 else pl.ds(0, 8)
        at = lambda a: OWN + (8 - a if dx > 0 else a - 1)
        keep = jnp.where(outside(dx, dy) == 0, 1.0, 0.0).astype(F32)
        tiles = corner_pack(lambda a: K0[at(a), rows], lambda a: R0[at(a), rows], dx > 0, dy > 0)
        for t, tile in enumerate(tiles):
            CS[i, t] = tile * keep

    fine, coarse = iotas(512, 128)
    to_quarter = zero_one(((fine // 256) == (coarse // 64)) & ((fine % 256) // 4 == coarse % 64))
    parts = [
        (K0[OWN + 4 * p, 0:16] + K0[OWN + 4 * p + 1, 0:16]) + (K0[OWN + 4 * p + 2, 0:16] + K0[OWN + 4 * p + 3, 0:16])
        for p in (0, 1)
    ]
    T0[0:16] = times_right(jnp.concatenate(parts, axis=1), to_quarter)
    quarter = (T0[pl.ds(0, 4, stride=4)] + T0[pl.ds(1, 4, stride=4)]) + (
        T0[pl.ds(2, 4, stride=4)] + T0[pl.ds(3, 4, stride=4)]
    )
    KS[...] = quarter * (1.0 / 64.0)

    pl.semaphore_wait(barrier, (nw - 1) + 3 * (nn - 1))

    halo = []

    def push(src, dst, to):
        i = len(halo)
        halo.append(remote(src, dst, halo_s.at[i], halo_r.at[i], to))
        halo[-1].start()

    for dx in (-1, 1):
        over = outside(dx, 0)
        for ref, width in ((K0, HALO_K), (R0, HALO_R)):
            start = OWN + 8 - width if dx > 0 else OWN
            land = OWN - width if dx > 0 else OWN + 8
            start = jnp.where(over == 1, PLANES, start)
            push(ref.at[pl.ds(start, width), 0:16], ref.at[land : land + width, 0:16], (wide(dx), n))
    for dy in (-1, 1):
        over = outside(0, dy)
        for ref in (K0, R0):
            start = jnp.where(over == 1, PLANES, OWN)
            rows = slice(8, 16) if dy > 0 else slice(0, 8)
            land = slice(24, 32) if dy > 0 else slice(16, 24)
            push(ref.at[pl.ds(start, 8), rows], ref.at[OWN : OWN + 8, land], (w, narrow(dy)))
    for i, (dx, dy) in enumerate(corners):
        push(CS.at[i], CR.at[3 - i], (wide(dx), narrow(dy)))

    def gather_k(d, carry):
        remote(KS, GK.at[n], kz_s.at[0], kz_r.at[0], (w, narrow(d))).start()
        return carry

    lax.fori_loop(1, nn, gather_k, 0)
    GK[n] = KS[...]

    for copy in halo:
        copy.wait_recv()
    for i, (dx, dy) in enumerate(corners):
        k, r = corner_unpack([CR[i, t] for t in range(5)], dy < 0)
        rows = pl.ds(24, 8) if dy < 0 else pl.ds(16, 8)
        at = lambda a: OWN - a if dx < 0 else OWN + 7 + a
        for a in range(1, 7):
            K0[at(a), rows] = k[a - 1]
        for a in range(1, 6):
            R0[at(a), rows] = r[a - 1]

    level0 = (WX, WY, WZ, DG)
    set_weights = weights(1, 21, K0, WX, WY, WZ, DG, IV)

    def first0(p):
        set_weights(p)
        EA[p] = IV[p] * R0[p]

    loop(1, 21, first0, False)

    def sweep0(source, target):
        def plane(p):
            target[p] = source[p] + IV[p] * (R0[p] - image_at(p, source, *level0))

        return plane

    loop(2, 20, sweep0(EA, EB), False)

    def residual0(i):
        p = 2 * i + 3
        XS[i] = (R0[p] - image_at(p, EB, *level0)) + (R0[p + 1] - image_at(p + 1, EB, *level0))

    loop(0, 8, residual0, False)
    halve = halve_z()
    T0[0:256] = times_right(XS[...].reshape(256, 256), halve)
    R1[1:9] = (0.5 * (T0[pl.ds(0, 128, stride=2)] + T0[pl.ds(1, 128, stride=2)])).reshape(8, 16, 128)
    k_pairs = jnp.concatenate([K0[2 * q + 1] + K0[2 * q + 2] for q in range(PLANES1)], axis=0)
    T0[...] = times_right(k_pairs, halve)
    K1[...] = (0.125 * (T0[pl.ds(0, 160, stride=2)] + T0[pl.ds(1, 160, stride=2)])).reshape(PLANES1, 16, 128)

    level1 = (WX1, WY1, WZ1, DG1)
    set_weights1 = weights(1, 9, K1, WX1, WY1, WZ1, DG1, IV1)

    def first1(q):
        set_weights1(q)
        A1[q] = IV1[q] * R1[q]

    def sweep1(source, target):
        def plane(q):
            target[q] = source[q] + IV1[q] * (R1[q] - image_at(q, source, *level1))

        return plane

    loop(1, 9, first1, True)
    loop(2, 8, sweep1(A1, B1), True)
    left = [R1[q] - image_at(q, B1, *level1) for q in range(OWN1, OWN1 + 4)]
    fine, coarse = iotas(256, 128)
    halve_pair = zero_one(((fine // 128) == (coarse // 64)) & ((fine % 128) // 2 == coarse % 64))
    pair = jnp.concatenate([(left[0] + left[1])[0:8], (left[2] + left[3])[0:8]], axis=1)
    pair = jnp.concatenate([pair, pair], axis=0)
    T0[0:16] = times_right(pair, halve_pair)
    SB2[0] = 0.5 * (T0[pl.ds(0, 4, stride=2)] + T0[pl.ds(1, 4, stride=2)])

    def gather_r(d, carry):
        for dx in (-1, 0, 1):
            src = SB2.at[outside(dx, 0)]
            remote(src, G2.at[(1 - dx) * nn + n], rz_s.at[0], rz_r.at[0], (wide(dx), narrow(d))).start()
        return carry

    lax.fori_loop(1, nn, gather_r, 0)
    for dx in (-1, 1):
        remote(SB2.at[outside(dx, 0)], G2.at[(1 - dx) * nn + n], rz_s.at[0], rz_r.at[0], (wide(dx), n)).start()
    G2[nn + n] = SB2[0]

    for x1 in range(4):
        E1S[0, x1, 0] = B1[OWN1 + x1, 0:8]
        E1S[0, x1, 1] = R1[OWN1 + x1, 0:8]
        E1S[0, x1, 2] = K1[OWN1 + x1, 0:8]
    around = [(dx, dy) for dx in (-1, 0, 1) for dy in (-1, 0, 1) if dx or dy]
    near = []
    for i, (dx, dy) in enumerate(around):
        src, dst = E1S.at[outside(dx, dy)], E1G.at[7 - i]
        planes = slice(1, 4) if dx > 0 else (slice(0, 3) if dx < 0 else slice(0, 4))
        arrays = slice(0, 3) if dx and dy else slice(0, 1)
        src, dst = src.at[planes, arrays], dst.at[planes, arrays]
        copy = remote(src, dst, e1_s.at[i], e1_r.at[i], (wide(dx), narrow(dy)))
        copy.start()
        near.append(copy)

    remote(GK.at[0 : nn - 1], GK.at[0 : nn - 1], kz_s.at[0], kz_r.at[0], (w, n)).wait_recv()
    for i in range(nn):
        K2X[0, 4 * i : 4 * i + 4] = GK[i]
    slab_k = K2X[0]
    beside = (-2, -1, 1, 2)
    kx = []
    for i, dx in enumerate(beside):
        copy = remote(K2X.at[outside(dx, 0)], K2S.at[2 - dx], kx_s.at[i], kx_r.at[i], (wide(dx), n))
        copy.start()
        kx.append(copy)
    K2S[2] = slab_k

    row, lane = iotas(32, 128)
    own_chunk = (row // 8) == (lane // 32)
    fine, coarse = iotas(128, 128)
    fold = zero_one((fine % 64) // 2 == coarse % 32)
    unfold = zero_one((coarse % 64) // 2 == fine % 32)

    def to_level3(x):
        spread = jnp.where(own_chunk, times_right(x, fold), 0.0)
        T1[...] = (spread[0:8] + spread[8:16]) + (spread[16:24] + spread[24:32])
        return T1[pl.ds(0, 4, stride=2)] + T1[pl.ds(1, 4, stride=2)]

    def to_all(src, dst, send, recv):
        def one(d, carry):
            remote(src, dst.at[w], send.at[0], recv.at[0], (wide(d), n)).start()
            return carry

        lax.fori_loop(1, nw, one, 0)
        dst[w] = src[...]

    def from_all(dst, send, recv):
        return remote(dst.at[0 : nw - 1], dst.at[0 : nw - 1], send.at[0], recv.at[0], (w, n))

    K3S[...] = 0.125 * to_level3(slab_k)
    to_all(K3S, K3G, k3_s, k3_r)

    for copy in kx:
        copy.wait_recv()
    k2 = K2S[...]
    row = lax.broadcasted_iota(jnp.int32, (5, 32, 128), 1)
    cell = lax.broadcasted_iota(jnp.int32, (5, 32, 128), 2)
    odd = cell >= 64
    cell = cell % 64
    none = jnp.zeros((1, 32, 128), F32)

    def above(v):
        turned = pltpu.roll(v, 64, 2)
        after = jnp.concatenate([turned[1:], none], axis=0)
        return jnp.where(odd[: v.shape[0]], after, turned)

    def below(v):
        turned = pltpu.roll(v, 64, 2)
        before = jnp.concatenate([none, turned[:-1]], axis=0)
        return jnp.where(odd[: v.shape[0]], turned, before)

    wx2 = 0.5 * (k2 + above(k2))
    wy2 = jnp.where(row == 31, 0.0, 0.5 * (k2 + pltpu.roll(k2, 31, 1)))
    wz2 = jnp.where(cell == 63, 0.0, 0.5 * (k2 + pltpu.roll(k2, 127, 2)))
    diag2 = (wx2 + below(wx2)) + (wy2 + pltpu.roll(wy2, 1, 1)) + (wz2 + pltpu.roll(wz2, 1, 2))
    diag2 += jnp.where((row == 0) | (row == 31), 0.5 * k2, 0.0) + jnp.where((cell == 0) | (cell == 63), 0.5 * k2, 0.0)
    inv2 = jnp.where(k2 > 0.0, OMEGA / diag2, 0.0)

    def image2(v, at):
        x, y, z = wx2[at], wy2[at], wz2[at]
        total = x * above(v) + below(x * v)
        total += y * pltpu.roll(v, 31, 1) + pltpu.roll(y * v, 1, 1)
        total += z * pltpu.roll(v, 127, 2) + pltpu.roll(z * v, 1, 2)
        return diag2[at] * v - total

    some = slice(1, 4)
    arrived = G2.at[0 : 3 * nn - 1]
    remote(arrived, arrived, rz_s.at[0], rz_r.at[0], (w, n)).wait_recv()
    r2 = jnp.concatenate(
        [jnp.concatenate([G2[b * nn + i] for i in range(nn)], axis=0)[None] for b in range(3)], axis=0
    )
    e2 = inv2[some] * r2
    e2 = e2 + inv2[some] * (r2 - image2(e2, some))
    left2 = (r2 - image2(e2, some))[1]
    R3S[...] = 0.5 * to_level3(left2)
    to_all(R3S, R3G, r3_s, r3_r)

    MB[0, 0] = e2[1]
    MB[0, 1] = r2[1]
    e2x = []
    for i, dx in enumerate(beside):
        copy = remote(MB.at[outside(dx, 0)], E2G.at[2 - dx], e2_s.at[i], e2_r.at[i], (wide(dx), n))
        copy.start()
        e2x.append(copy)
    E2G[2] = MB[0]

    for copy in near:
        copy.wait_recv()
    sub = lax.broadcasted_iota(jnp.int32, (8, 128), 0)

    def rim1(x1, which):
        dx = -1 if x1 < 0 else (1 if x1 > 3 else 0)
        after, before = around.index((dx, 1)), around.index((dx, -1))
        return jnp.where(sub < 4, E1G[after, x1 - 4 * dx, which], E1G[before, x1 - 4 * dx, which])

    for x1 in (-3, -2, -1, 4, 5, 6):
        K1[OWN1 + x1, 8:16] = rim1(x1, 2)
        if -2 <= x1 <= 5:
            R1[OWN1 + x1, 8:16] = rim1(x1, 1)
    loop(1, 9, set_weights1, True)

    from_all(K3G, k3_s, k3_r).wait_recv()

    def in_order(gathered, target):
        for i in range(nw):
            F3[4 * i : 4 * i + 4] = gathered[i]
        for j in range(4):
            target[j] = F3[pl.ds(j, nw, stride=4)]

    in_order(K3G, P3)
    row, lane = iotas(nw, 128)
    last_chunk, first_chunk = lane >= 96, lane < 32
    for j in range(4):
        here = P3[j]
        X3[j] = jnp.where(row == nw - 1, 0.0, 0.5 * (here + pltpu.roll(here, nw - 1, 0)))
        Z3[j] = jnp.where(lane % 32 == 31, 0.0, 0.5 * (here + pltpu.roll(here, 127, 1)))
        if j < 3:
            Y3[j] = 0.5 * (here + P3[j + 1])
        else:
            Y3[j] = jnp.where(last_chunk, 0.0, 0.5 * (here + pltpu.roll(P3[0], 96, 1)))
    for j in range(4):
        here = P3[j]
        lower = Y3[j - 1] if j else pltpu.roll(Y3[3], 32, 1)
        d = (X3[j] + pltpu.roll(X3[j], 1, 0)) + (Y3[j] + lower) + (Z3[j] + pltpu.roll(Z3[j], 1, 1))
        rim = jnp.where((row == 0) | (row == nw - 1), 0.5, 0.0)
        rim += jnp.where((lane % 32 == 0) | (lane % 32 == 31), 0.5, 0.0)
        if j == 0:
            rim += jnp.where(first_chunk, 0.5, 0.0)
        if j == 3:
            rim += jnp.where(last_chunk, 0.5, 0.0)
        D3[j] = d + rim * here

    from_all(R3G, r3_s, r3_r).wait_recv()
    in_order(R3G, Q3)
    norm = jnp.zeros((nw, 128), F32)
    for j in range(4):
        P3[j] = Q3[j]
        S3[j] = jnp.zeros((nw, 128), F32)
        norm += Q3[j] * Q3[j]
    norm = jnp.sum(norm, keepdims=True)

    def iteration(step, norm):
        images = []
        dot = jnp.zeros((nw, 128), F32)
        carried = pltpu.roll(Y3[3] * P3[3], 32, 1)
        for j in range(4):
            v = P3[j]
            x, y, z = X3[j], Y3[j], Z3[j]
            total = x * pltpu.roll(v, nw - 1, 0) + pltpu.roll(x * v, 1, 0)
            total += z * pltpu.roll(v, 127, 1) + pltpu.roll(z * v, 1, 1)
            total += y * (P3[j + 1] if j < 3 else pltpu.roll(P3[0], 96, 1)) + carried
            carried = y * v
            image = D3[j] * v - total
            images.append(image)
            dot += v * image
        alpha = norm / jnp.sum(dot, keepdims=True)
        following = jnp.zeros((nw, 128), F32)
        for j in range(4):
            S3[j] = S3[j] + alpha * P3[j]
            rest = Q3[j] - alpha * images[j]
            Q3[j] = rest
            following += rest * rest
        following = jnp.sum(following, keepdims=True)
        beta = following / norm
        for j in range(4):
            P3[j] = Q3[j] + beta * P3[j]
        return following

    lax.fori_loop(0, COARSE_ITERS, iteration, norm)
    for j in range(4):
        E3[j, 8 : 8 + nw] = S3[j]

    for i in range(5):
        for j in range(4):
            DS[8 * i + 2 * j : 8 * i + 2 * j + 2] = jnp.broadcast_to(E3[j, pl.ds(w + (6 + i), 1)], (2, 128))
    chunk = lax.broadcasted_iota(jnp.int32, (8, 128), 1) // 32
    rows = [jnp.where(chunk == c, DS[8 * i : 8 * i + 8], 0.0) for i in range(5) for c in range(4)]
    added = times_right(jnp.concatenate(rows, axis=0), unfold).reshape(5, 32, 128)
    for copy in e2x:
        copy.wait_recv()
    r2 = E2G[:, 1]
    e2 = E2G[:, 0] + added
    every = slice(0, 5)
    e2 = e2 + inv2 * (r2 - image2(e2, every))
    e2 = e2 + inv2 * (r2 - image2(e2, every))

    coarse, fine = iotas(128, 256)
    double_pair = zero_one(((fine // 128) == (coarse // 64)) & ((fine % 128) // 2 == coarse % 64))
    stretched = times_right(e2[1:4].reshape(96, 128), double_pair)
    i, y2 = iotas(16, 32)
    y1 = 8 * n + jnp.where(i < 12, i, i - 16)
    pick = zero_one((y1 == 2 * y2) | (y1 == 2 * y2 + 1))
    for b in range(3):
        grown = times_left(pick, stretched[32 * b : 32 * b + 32])
        for p in range(2):
            x2 = 2 * (b - 1) + p
            for x1 in (2 * x2, 2 * x2 + 1):
                if -3 <= x1 <= 6:
                    dx = -1 if x1 < 0 else (1 if x1 > 3 else 0)
                    mine = E1G[around.index((dx, 0)), x1 - 4 * dx, 0] if dx else B1[OWN1 + x1, 0:8]
                    rim = rim1(x1, 0)
                    A1[OWN1 + x1, 0:8] = mine + grown[0:8, 128 * p : 128 * p + 128]
                    A1[OWN1 + x1, 8:16] = rim + grown[8:16, 128 * p : 128 * p + 128]
    loop(1, 9, sweep1(A1, B1), True)
    loop(2, 8, sweep1(B1, A1), True)

    stretched = times_right(A1[2:8].reshape(96, 128), double_z())
    i, j = iotas(32, 16)
    twice = zero_one(i // 2 == j)
    for q in range(6):
        grown = times_left(twice, stretched[16 * q : 16 * q + 16])
        for p in (5 + 2 * q, 6 + 2 * q):
            EA[p] = EB[p] + grown
    loop(6, 16, sweep0(EA, EB), False)

    def last(p):
        value = EB[p] + IV[p] * (R0[p] - image_at(p, EB, *level0))
        out[p - OWN] = value[0:16]

    loop(7, 15, last, False)

    for copy in halo + near + kx + e2x:
        copy.wait_send()
    remote(GK.at[0 : nn - 1], GK.at[0 : nn - 1], kz_s.at[0], kz_r.at[0], (w, n)).wait_send()
    remote(arrived, arrived, rz_s.at[0], rz_r.at[0], (w, n)).wait_send()
    from_all(K3G, k3_s, k3_r).wait_send()
    from_all(R3G, r3_s, r3_r).wait_send()


def solution(mesh):
    nw, nn = mesh.shape["wide"], mesh.shape["narrow"]

    def per_device(right_side, coefficient):
        fine = pltpu.VMEM((PLANES, 32, 256), F32)
        with_zeros = pltpu.VMEM((PLANES + 8, 32, 256), F32)
        middle = pltpu.VMEM((PLANES1, 16, 128), F32)
        coarse = pltpu.VMEM((4, nw, 128), F32)
        vmem = lambda *shape: pltpu.VMEM(shape, F32)
        dma = lambda count: pltpu.SemaphoreType.DMA((count,))
        scratch = [with_zeros, with_zeros] + [fine] * 7
        scratch += [vmem(8, 32, 256), vmem(4, 5, 8, 256), vmem(4, 5, 8, 256), vmem(320, 128)]
        scratch += [middle] * 9 + [vmem(2, 4, 3, 8, 128), vmem(8, 4, 3, 8, 128), vmem(8, 128)]
        scratch += [vmem(2, 4, 128), vmem(3 * nn, 4, 128), vmem(4, 128), vmem(nn, 4, 128)]
        scratch += [vmem(2, 32, 128), vmem(5, 32, 128)]
        scratch += [vmem(4, 128), vmem(nw, 4, 128), vmem(4, 128), vmem(nw, 4, 128), vmem(4 * nw, 128)]
        scratch += [coarse] * 7
        scratch += [vmem(2, 2, 32, 128), vmem(5, 2, 32, 128), vmem(4, nw + 16, 128), vmem(40, 128)]
        scratch += [dma(2), dma(12), dma(12), dma(1), dma(1), dma(1), dma(1), dma(4), dma(4), dma(8), dma(8)]
        scratch += [dma(1), dma(1), dma(1), dma(1), dma(4), dma(4)]
        return pl.pallas_call(
            functools.partial(kernel, nw, nn),
            out_shape=jax.ShapeDtypeStruct((8, 16, 256), F32),
            in_specs=[pl.BlockSpec(memory_space=pl.ANY)] * 2,
            out_specs=pl.BlockSpec(memory_space=pltpu.VMEM),
            scratch_shapes=scratch,
            compiler_params=pltpu.CompilerParams(
                collective_id=0, has_side_effects=True, vmem_limit_bytes=40 * 1024 * 1024
            ),
        )(right_side, coefficient)

    placed = P("wide", "narrow", None)
    return jax.shard_map(per_device, mesh=mesh, in_specs=(placed, placed), out_specs=placed, check_vma=False)
```

```python
import functools

import jax
import jax.numpy as jnp
from jax import lax
from jax.experimental import pallas as pl
from jax.experimental.pallas import tpu as pltpu
from jax.sharding import PartitionSpec as P

COARSE_ITERS = 5
OMEGA = 0.8
MESH = pl.DeviceIdType.MESH
F32 = jnp.float32

OWN = 7
PLANES = 22
HALO_K, HALO_R = 7, 6
BY_WEIGHTS, BY_FIRST, BY_SWEEP, BY_RESIDUAL, BY_LAST = 4, 10, 3, 2, 4
OWN1 = 3
PLANES1 = 10


def split(x):
    high = x.astype(jnp.bfloat16)
    rest = x - high.astype(F32)
    middle = rest.astype(jnp.bfloat16)
    low = (rest - middle.astype(F32)).astype(jnp.bfloat16)
    return high, middle, low


def times_right(x, zero_one):
    rows = x.shape[0]
    out = jnp.dot(jnp.concatenate(split(x), axis=0), zero_one, preferred_element_type=F32)
    return out[:rows] + out[rows : 2 * rows] + out[2 * rows :]


def times_left(zero_one, x):
    columns = x.shape[1]
    out = jnp.dot(zero_one, jnp.concatenate(split(x), axis=1), preferred_element_type=F32)
    return out[:, :columns] + out[:, columns : 2 * columns] + out[:, 2 * columns :]


def iotas(rows, columns):
    shape = (rows, columns)
    return lax.broadcasted_iota(jnp.int32, shape, 0), lax.broadcasted_iota(jnp.int32, shape, 1)


def zero_one(condition):
    return jnp.where(condition, 1.0, 0.0).astype(jnp.bfloat16)


def halve_z():
    fine, coarse = iotas(256, 128)
    return zero_one(fine // 2 == coarse)


def double_z():
    coarse, fine = iotas(128, 256)
    return zero_one(fine // 2 == coarse)


def reciprocal(x):
    guess = pl.reciprocal(x, approx=True)
    return guess * (2.0 - x * guess)


def weights(k, wx, wy, wz, diag, inv):
    rows, columns = k.shape[1:]
    lane = lax.broadcasted_iota(jnp.int32, (rows, columns), 1)
    rim = jnp.where((lane == 0) | (lane == columns - 1), 0.5, 0.0)
    half = jnp.where(lane == columns - 1, 0.0, 0.5)

    def plane(p):
        here = k[p]
        x = 0.5 * (here + k[p + 1])
        lower = 0.5 * (here + k[p - 1])
        y = 0.5 * (here + pltpu.roll(here, rows - 1, 0))
        z = half * (here + pltpu.roll(here, columns - 1, 1))
        d = (x + lower) + (y + pltpu.roll(y, 1, 0)) + (z + pltpu.roll(z, 1, 1)) + rim * here
        wx[p] = x
        wy[p] = y
        wz[p] = z
        diag[p] = d
        inv[p] = jnp.where(here > 0.0, OMEGA * reciprocal(d), 0.0)

    return plane


def pull_at(p, v, wx, wy, wz, keep=None):
    rows, columns = v.shape[1:]
    keep = rows if keep is None else keep
    here = v[p]
    y, z = wy[p], wz[p]
    total = wx[p, :keep] * v[p + 1, :keep] + wx[p - 1, :keep] * v[p - 1, :keep]
    total += y[:keep] * pltpu.roll(here, rows - 1, 0)[:keep] + pltpu.roll(y * here, 1, 0)[:keep]
    here, z = here[:keep], z[:keep]
    total += z * pltpu.roll(here, columns - 1, 1) + pltpu.roll(z * here, 1, 1)
    return total


def loop(first, last, body, by):
    if last - first <= by:
        for p in range(first, last):
            body(p)
        return

    def step(i, carry):
        for p in range(by):
            body(first + i * by + p)
        return carry

    whole = (last - first) // by
    lax.fori_loop(0, whole, step, 0)
    for p in range(first + whole * by, last):
        body(p)


def turns(y_low):
    return lambda x, by: pltpu.roll(x, (by if y_low else -by) % 8, 0)


def from_corner(y_low):
    sub = lax.broadcasted_iota(jnp.int32, (8, 256), 0)
    return 7 - sub if y_low else sub


def pack_k(k, y_low):
    near, turn = from_corner(y_low), turns(y_low)
    return [
        jnp.where(near < 6, k[0], turn(k[4], 2)),
        jnp.where(near < 5, k[1], turn(k[3], 3)),
        jnp.where(near < 4, k[2], turn(k[5], 4)),
    ]


def unpack_k(tiles, y_low):
    turn = turns(y_low)
    one, two, three = tiles
    return [one, two, three, turn(two, -3), turn(one, -2), turn(three, -4)]


def pack_r(r, y_low):
    near, turn = from_corner(y_low), turns(y_low)
    return [
        jnp.where(near < 5, r[0], turn(r[2], 3)),
        jnp.where(near < 4, r[1], jnp.where(near >= 6, turn(r[3], 2), turn(r[4], 4))),
    ]


def unpack_r(tiles, y_low):
    turn = turns(y_low)
    one, two = tiles
    return [one, two, turn(one, -3), turn(two, -2), turn(two, -4)]


def kernel(nw, nn, r_in, k_in, out, *refs):
    (K0, R0, EA, EB, WX, WY, WZ, DG, IV, XS, CK, CKR, CR, CRR, T0, OUT,
     K1, R1, A1, B1, WX1, WY1, WZ1, DG1, IV1, E1S, E1G, T1,
     SB2, G2, KS, GK, K2X, K2S, K3S, K3G, R3S, R3G, F3,
     X3, Y3, Z3, D3, S3, Q3, P3, MB, E2G, E3, DS,
     load, halo_s, halo_r, tail_s, tail_r, kz_s, kz_r, rz_s, rz_r, kx_s, kx_r, e1_s, e1_r,
     k3_s, k3_r, k4_s, k4_r, r3_s, r3_r, e2_s, e2_r) = refs
    w, n = lax.axis_index("wide"), lax.axis_index("narrow")
    wide = lambda d: lax.rem(w + (d + nw), nw)
    narrow = lambda d: lax.rem(n + (d + nn), nn)

    def outside(dx, dy):
        over = jnp.int32(0)
        if dx:
            over = over + jnp.where(w == (nw - 1 if dx > 0 else 0), 1, 0)
            if abs(dx) == 2:
                over = over + jnp.where(w == (nw - 2 if dx > 0 else 1), 1, 0)
        if dy:
            over = over + jnp.where(n == (nn - 1 if dy > 0 else 0), 1, 0)
        return jnp.where(over > 0, 1, 0)

    def remote(src, dst, send, recv, to):
        return pltpu.make_async_remote_copy(
            src_ref=src, dst_ref=dst, send_sem=send, recv_sem=recv, device_id=to, device_id_type=MESH
        )

    load_k = pltpu.make_async_copy(k_in, K0.at[OWN : OWN + 8, 0:16], load.at[0])
    load_r = pltpu.make_async_copy(r_in, R0.at[OWN : OWN + 8, 0:16], load.at[1])
    load_k.start()
    load_r.start()
    barrier = pltpu.get_barrier_semaphore()

    def greet_wide(d, carry):
        pl.semaphore_signal(barrier, inc=1, device_id=(wide(d), n), device_id_type=MESH)
        return carry

    def greet_narrow(d, carry):
        for dx in (-1, 0, 1):
            pl.semaphore_signal(barrier, inc=1, device_id=(wide(dx), narrow(d)), device_id_type=MESH)
        return carry

    lax.fori_loop(1, nn, greet_narrow, 0)
    lax.fori_loop(1, nw, greet_wide, 0)

    zero_planes = jnp.zeros((8, 16, 256), F32)
    K0[PLANES : PLANES + 8, 0:16] = zero_planes
    R0[PLANES : PLANES + 8, 0:16] = zero_planes
    zero_rows = jnp.zeros((16, 256), F32)
    for p in (0, 21):
        K0[p, 16:32] = zero_rows
    for p in (1, 20):
        R0[p, 16:32] = zero_rows
    SB2[1] = jnp.zeros((4, 128), F32)
    K2X[1] = jnp.zeros((32, 128), F32)
    MB[1] = jnp.zeros((2, 32, 128), F32)
    E1S[1] = jnp.zeros((4, 3, 8, 128), F32)
    E3[...] = jnp.zeros((4, nw + 16, 128), F32)
    load_k.wait()
    load_r.wait()

    corners = [(dx, dy) for dx in (-1, 1) for dy in (-1, 1)]
    for i, (dx, dy) in enumerate(corners):
        rows = pl.ds(8, 8) if dy > 0 else pl.ds(0, 8)
        at = lambda a: OWN + (8 - a if dx > 0 else a - 1)
        keep = jnp.where(outside(dx, dy) == 0, 1.0, 0.0).astype(F32)
        for t, tile in enumerate(pack_k([K0[at(a), rows] for a in range(1, 7)], dy > 0)):
            CK[i, t] = tile * keep
        for t, tile in enumerate(pack_r([R0[at(a), rows] for a in range(1, 6)], dy > 0)):
            CR[i, t] = tile * keep

    fine, coarse = iotas(512, 128)
    to_quarter = zero_one(((fine // 256) == (coarse // 64)) & ((fine % 256) // 4 == coarse % 64))
    parts = [
        (K0[OWN + 4 * p, 0:16] + K0[OWN + 4 * p + 1, 0:16]) + (K0[OWN + 4 * p + 2, 0:16] + K0[OWN + 4 * p + 3, 0:16])
        for p in (0, 1)
    ]
    T0[0:16] = times_right(jnp.concatenate(parts, axis=1), to_quarter)
    quarter = (T0[pl.ds(0, 4, stride=4)] + T0[pl.ds(1, 4, stride=4)]) + (
        T0[pl.ds(2, 4, stride=4)] + T0[pl.ds(3, 4, stride=4)]
    )
    KS[...] = quarter * (1.0 / 64.0)

    pl.semaphore_wait(barrier, (nw - 1) + 3 * (nn - 1))

    def send_halo(ref, width, packed, landing, send, recv):
        copies = []

        def push(src, dst, to):
            i = len(copies)
            copies.append(remote(src, dst, send.at[i], recv.at[i], to))
            copies[-1].start()

        for dy in (-1, 1):
            start = jnp.where(outside(0, dy) == 1, PLANES, OWN)
            rows = slice(8, 16) if dy > 0 else slice(0, 8)
            land = slice(24, 32) if dy > 0 else slice(16, 24)
            push(ref.at[pl.ds(start, 8), rows], ref.at[OWN : OWN + 8, land], (w, narrow(dy)))
        for dx in (-1, 1):
            start = OWN + 8 - width if dx > 0 else OWN
            land = OWN - width if dx > 0 else OWN + 8
            start = jnp.where(outside(dx, 0) == 1, PLANES, start)
            push(ref.at[pl.ds(start, width), 0:16], ref.at[land : land + width, 0:16], (wide(dx), n))
        for i, (dx, dy) in enumerate(corners):
            push(packed.at[i], landing.at[3 - i], (wide(dx), narrow(dy)))
        return copies

    def place_corners(ref, landing, unpack, count):
        for i, (dx, dy) in enumerate(corners):
            tiles = unpack([landing[i, t] for t in range(count)], dy < 0)
            rows = pl.ds(24, 8) if dy < 0 else pl.ds(16, 8)
            for a, tile in enumerate(tiles, 1):
                ref[OWN - a if dx < 0 else OWN + 7 + a, rows] = tile

    halo = send_halo(K0, HALO_K, CK, CKR, halo_s, halo_r)
    tail = send_halo(R0, HALO_R, CR, CRR, tail_s, tail_r)

    def gather_k(d, carry):
        remote(KS, GK.at[n], kz_s.at[0], kz_r.at[0], (w, narrow(d))).start()
        return carry

    lax.fori_loop(1, nn, gather_k, 0)
    GK[n] = KS[...]

    for copy in halo:
        copy.wait_recv()
    place_corners(K0, CKR, unpack_k, 3)
    WX[0] = 0.5 * (K0[0] + K0[1])
    loop(1, 21, weights(K0, WX, WY, WZ, DG, IV), BY_WEIGHTS)

    remote(GK.at[0 : nn - 1], GK.at[0 : nn - 1], kz_s.at[0], kz_r.at[0], (w, n)).wait_recv()
    for i in range(nn):
        K2X[0, 4 * i : 4 * i + 4] = GK[i]
    slab_k = K2X[0]
    beside = (-2, -1, 1, 2)
    kx = []
    for i, dx in enumerate(beside):
        copy = remote(K2X.at[outside(dx, 0)], K2S.at[2 - dx], kx_s.at[i], kx_r.at[i], (wide(dx), n))
        copy.start()
        kx.append(copy)
    K2S[2] = slab_k

    row, lane = iotas(32, 128)
    own_chunk = (row // 8) == (lane // 32)
    fine, coarse = iotas(128, 128)
    fold = zero_one((fine % 64) // 2 == coarse % 32)
    unfold = zero_one((coarse % 64) // 2 == fine % 32)

    def to_level3(x):
        spread = jnp.where(own_chunk, times_right(x, fold), 0.0)
        T1[...] = (spread[0:8] + spread[8:16]) + (spread[16:24] + spread[24:32])
        return T1[pl.ds(0, 4, stride=2)] + T1[pl.ds(1, 4, stride=2)]

    ny = nw // 8
    in_row, in_column = lax.rem(w, 8), w // 8
    K3S[...] = 0.125 * to_level3(slab_k)

    def along_y(d, carry):
        remote(K3S, K3G.at[in_row, in_column], k3_s.at[0], k3_r.at[0], (wide(8 * d), n)).start()
        return carry

    lax.fori_loop(1, ny, along_y, 0)
    K3G[in_row, in_column] = K3S[...]

    for copy in tail:
        copy.wait_recv()
    place_corners(R0, CRR, unpack_r, 2)

    level0 = (WX, WY, WZ)

    def first0(p):
        EA[p] = IV[p] * R0[p]

    loop(1, 21, first0, BY_FIRST)

    def sweep0(source, target):
        def plane(p):
            target[p] = (1.0 - OMEGA) * source[p] + IV[p] * (R0[p] + pull_at(p, source, *level0))

        return plane

    loop(2, 20, sweep0(EA, EB), BY_SWEEP)

    def residual0(i):
        p = 2 * i + 3
        one, two = ((R0[q] - DG[q] * EB[q]) + pull_at(q, EB, *level0) for q in (p, p + 1))
        XS[i] = one + two

    loop(0, 8, residual0, BY_RESIDUAL)
    halve = halve_z()
    T0[0:256] = times_right(XS[...].reshape(256, 256), halve)
    R1[1:9] = (0.5 * (T0[pl.ds(0, 128, stride=2)] + T0[pl.ds(1, 128, stride=2)])).reshape(8, 16, 128)
    k_pairs = jnp.concatenate([K0[2 * q + 1] + K0[2 * q + 2] for q in range(PLANES1)], axis=0)
    T0[...] = times_right(k_pairs, halve)
    K1[...] = (0.125 * (T0[pl.ds(0, 160, stride=2)] + T0[pl.ds(1, 160, stride=2)])).reshape(PLANES1, 16, 128)

    level1 = (WX1, WY1, WZ1)
    set_weights1 = weights(K1, WX1, WY1, WZ1, DG1, IV1)

    def sweep1(source, target):
        def plane(q):
            target[q] = (1.0 - OMEGA) * source[q] + IV1[q] * (R1[q] + pull_at(q, source, *level1))

        return plane

    WX1[0] = 0.5 * (K1[0] + K1[1])
    for q in range(1, 9):
        set_weights1(q)
        A1[q] = IV1[q] * R1[q]
    loop(2, 8, sweep1(A1, B1), 8)
    left = [(R1[q] - DG1[q] * B1[q]) + pull_at(q, B1, *level1) for q in range(OWN1, OWN1 + 4)]
    fine, coarse = iotas(256, 128)
    halve_pair = zero_one(((fine // 128) == (coarse // 64)) & ((fine % 128) // 2 == coarse % 64))
    pair = jnp.concatenate([(left[0] + left[1])[0:8], (left[2] + left[3])[0:8]], axis=1)
    pair = jnp.concatenate([pair, pair], axis=0)
    T0[0:16] = times_right(pair, halve_pair)
    SB2[0] = 0.5 * (T0[pl.ds(0, 4, stride=2)] + T0[pl.ds(1, 4, stride=2)])

    def gather_r(d, carry):
        for dx in (-1, 0, 1):
            src = SB2.at[outside(dx, 0)]
            remote(src, G2.at[(1 - dx) * nn + n], rz_s.at[0], rz_r.at[0], (wide(dx), narrow(d))).start()
        return carry

    lax.fori_loop(1, nn, gather_r, 0)
    for dx in (-1, 1):
        remote(SB2.at[outside(dx, 0)], G2.at[(1 - dx) * nn + n], rz_s.at[0], rz_r.at[0], (wide(dx), n)).start()
    G2[nn + n] = SB2[0]

    for x1 in range(4):
        E1S[0, x1, 0] = B1[OWN1 + x1, 0:8]
        E1S[0, x1, 1] = R1[OWN1 + x1, 0:8]
        E1S[0, x1, 2] = K1[OWN1 + x1, 0:8]
    around = [(dx, dy) for dx in (-1, 0, 1) for dy in (-1, 0, 1) if dx or dy]
    near = []
    for i, (dx, dy) in enumerate(around):
        src, dst = E1S.at[outside(dx, dy)], E1G.at[7 - i]
        planes = slice(1, 4) if dx > 0 else (slice(0, 3) if dx < 0 else slice(0, 4))
        arrays = slice(0, 3) if dx and dy else slice(0, 1)
        src, dst = src.at[planes, arrays], dst.at[planes, arrays]
        copy = remote(src, dst, e1_s.at[i], e1_r.at[i], (wide(dx), narrow(dy)))
        copy.start()
        near.append(copy)

    column = K3G.at[0, 0 : ny - 1]
    remote(column, column, k3_s.at[0], k3_r.at[0], (w, n)).wait_recv()

    def along_row(d, carry):
        to = 8 * in_column + lax.rem(in_row + d, 8)
        remote(K3G.at[in_row], K3G.at[in_row], k4_s.at[0], k4_r.at[0], (to, n)).start()
        return carry

    lax.fori_loop(1, 8, along_row, 0)

    def to_all(src, dst, send, recv):
        def one(d, carry):
            remote(src, dst.at[w], send.at[0], recv.at[0], (wide(d), n)).start()
            return carry

        lax.fori_loop(1, nw, one, 0)
        dst[w] = src[...]

    def from_all(dst, send, recv):
        return remote(dst.at[0 : nw - 1], dst.at[0 : nw - 1], send.at[0], recv.at[0], (w, n))

    for copy in kx:
        copy.wait_recv()
    k2 = K2S[...]
    row = lax.broadcasted_iota(jnp.int32, (5, 32, 128), 1)
    cell = lax.broadcasted_iota(jnp.int32, (5, 32, 128), 2)
    odd = cell >= 64
    cell = cell % 64
    none = jnp.zeros((1, 32, 128), F32)

    def above(v):
        turned = pltpu.roll(v, 64, 2)
        after = jnp.concatenate([turned[1:], none], axis=0)
        return jnp.where(odd[: v.shape[0]], after, turned)

    def below(v):
        turned = pltpu.roll(v, 64, 2)
        before = jnp.concatenate([none, turned[:-1]], axis=0)
        return jnp.where(odd[: v.shape[0]], turned, before)

    wx2 = 0.5 * (k2 + above(k2))
    wy2 = jnp.where(row == 31, 0.0, 0.5 * (k2 + pltpu.roll(k2, 31, 1)))
    wz2 = jnp.where(cell == 63, 0.0, 0.5 * (k2 + pltpu.roll(k2, 127, 2)))
    diag2 = (wx2 + below(wx2)) + (wy2 + pltpu.roll(wy2, 1, 1)) + (wz2 + pltpu.roll(wz2, 1, 2))
    diag2 += jnp.where((row == 0) | (row == 31), 0.5 * k2, 0.0) + jnp.where((cell == 0) | (cell == 63), 0.5 * k2, 0.0)
    inv2 = jnp.where(k2 > 0.0, OMEGA / diag2, 0.0)

    def image2(v, at):
        x, y, z = wx2[at], wy2[at], wz2[at]
        total = x * above(v) + below(x * v)
        total += y * pltpu.roll(v, 31, 1) + pltpu.roll(y * v, 1, 1)
        total += z * pltpu.roll(v, 127, 2) + pltpu.roll(z * v, 1, 2)
        return diag2[at] * v - total

    some = slice(1, 4)
    arrived = G2.at[0 : 3 * nn - 1]
    remote(arrived, arrived, rz_s.at[0], rz_r.at[0], (w, n)).wait_recv()
    r2 = jnp.concatenate(
        [jnp.concatenate([G2[b * nn + i] for i in range(nn)], axis=0)[None] for b in range(3)], axis=0
    )
    e2 = inv2[some] * r2
    e2 = e2 + inv2[some] * (r2 - image2(e2, some))
    left2 = (r2 - image2(e2, some))[1]
    R3S[...] = 0.5 * to_level3(left2)
    to_all(R3S, R3G, r3_s, r3_r)

    MB[0, 0] = e2[1]
    MB[0, 1] = r2[1]
    e2x = []
    for i, dx in enumerate(beside):
        copy = remote(MB.at[outside(dx, 0)], E2G.at[2 - dx], e2_s.at[i], e2_r.at[i], (wide(dx), n))
        copy.start()
        e2x.append(copy)
    E2G[2] = MB[0]

    for copy in near:
        copy.wait_recv()
    sub = lax.broadcasted_iota(jnp.int32, (8, 128), 0)

    def rim1(x1, which):
        dx = -1 if x1 < 0 else (1 if x1 > 3 else 0)
        after, before = around.index((dx, 1)), around.index((dx, -1))
        return jnp.where(sub < 4, E1G[after, x1 - 4 * dx, which], E1G[before, x1 - 4 * dx, which])

    for x1 in (-3, -2, -1, 4, 5, 6):
        K1[OWN1 + x1, 8:16] = rim1(x1, 2)
        if -2 <= x1 <= 5:
            R1[OWN1 + x1, 8:16] = rim1(x1, 1)
    WX1[0] = 0.5 * (K1[0] + K1[1])
    loop(1, 9, set_weights1, 8)

    remote(K3G.at[0:7], K3G.at[0:7], k4_s.at[0], k4_r.at[0], (w, n)).wait_recv()

    def in_order(gathered, target):
        for i in range(nw):
            F3[4 * i : 4 * i + 4] = gathered(i)
        for j in range(4):
            target[j] = F3[pl.ds(j, nw, stride=4)]

    in_order(lambda i: K3G[i % 8, i // 8], P3)
    row, lane = iotas(nw, 128)
    last_chunk, first_chunk = lane >= 96, lane < 32
    for j in range(4):
        here = P3[j]
        X3[j] = jnp.where(row == nw - 1, 0.0, 0.5 * (here + pltpu.roll(here, nw - 1, 0)))
        Z3[j] = jnp.where(lane % 32 == 31, 0.0, 0.5 * (here + pltpu.roll(here, 127, 1)))
        if j < 3:
            Y3[j] = 0.5 * (here + P3[j + 1])
        else:
            Y3[j] = jnp.where(last_chunk, 0.0, 0.5 * (here + pltpu.roll(P3[0], 96, 1)))
    for j in range(4):
        here = P3[j]
        lower = Y3[j - 1] if j else pltpu.roll(Y3[3], 32, 1)
        d = (X3[j] + pltpu.roll(X3[j], 1, 0)) + (Y3[j] + lower) + (Z3[j] + pltpu.roll(Z3[j], 1, 1))
        rim = jnp.where((row == 0) | (row == nw - 1), 0.5, 0.0)
        rim += jnp.where((lane % 32 == 0) | (lane % 32 == 31), 0.5, 0.0)
        if j == 0:
            rim += jnp.where(first_chunk, 0.5, 0.0)
        if j == 3:
            rim += jnp.where(last_chunk, 0.5, 0.0)
        D3[j] = d + rim * here

    from_all(R3G, r3_s, r3_r).wait_recv()
    in_order(lambda i: R3G[i], Q3)
    norm = jnp.zeros((nw, 128), F32)
    for j in range(4):
        P3[j] = Q3[j]
        S3[j] = jnp.zeros((nw, 128), F32)
        norm += Q3[j] * Q3[j]
    norm = jnp.sum(norm, keepdims=True)

    def iteration(step, norm):
        images = []
        dot = jnp.zeros((nw, 128), F32)
        carried = pltpu.roll(Y3[3] * P3[3], 32, 1)
        for j in range(4):
            v = P3[j]
            x, y, z = X3[j], Y3[j], Z3[j]
            total = x * pltpu.roll(v, nw - 1, 0) + pltpu.roll(x * v, 1, 0)
            total += z * pltpu.roll(v, 127, 1) + pltpu.roll(z * v, 1, 1)
            total += y * (P3[j + 1] if j < 3 else pltpu.roll(P3[0], 96, 1)) + carried
            carried = y * v
            image = D3[j] * v - total
            images.append(image)
            dot += v * image
        alpha = norm / jnp.sum(dot, keepdims=True)
        following = jnp.zeros((nw, 128), F32)
        for j in range(4):
            S3[j] = S3[j] + alpha * P3[j]
            rest = Q3[j] - alpha * images[j]
            Q3[j] = rest
            following += rest * rest
        following = jnp.sum(following, keepdims=True)
        beta = following / norm
        for j in range(4):
            P3[j] = Q3[j] + beta * P3[j]
        return following

    lax.fori_loop(0, COARSE_ITERS, iteration, norm)
    for j in range(4):
        E3[j, 8 : 8 + nw] = S3[j]

    for i in range(5):
        for j in range(4):
            DS[8 * i + 2 * j : 8 * i + 2 * j + 2] = jnp.broadcast_to(E3[j, pl.ds(w + (6 + i), 1)], (2, 128))
    chunk = lax.broadcasted_iota(jnp.int32, (8, 128), 1) // 32
    rows = [jnp.where(chunk == c, DS[8 * i : 8 * i + 8], 0.0) for i in range(5) for c in range(4)]
    added = times_right(jnp.concatenate(rows, axis=0), unfold).reshape(5, 32, 128)
    for copy in e2x:
        copy.wait_recv()
    r2 = E2G[:, 1]
    e2 = E2G[:, 0] + added
    every = slice(0, 5)
    e2 = e2 + inv2 * (r2 - image2(e2, every))
    e2 = e2 + inv2 * (r2 - image2(e2, every))

    coarse, fine = iotas(128, 256)
    double_pair = zero_one(((fine // 128) == (coarse // 64)) & ((fine % 128) // 2 == coarse % 64))
    stretched = times_right(e2[1:4].reshape(96, 128), double_pair)
    i, y2 = iotas(16, 32)
    y1 = 8 * n + jnp.where(i < 12, i, i - 16)
    pick = zero_one((y1 == 2 * y2) | (y1 == 2 * y2 + 1))
    for b in range(3):
        grown = times_left(pick, stretched[32 * b : 32 * b + 32])
        for p in range(2):
            x2 = 2 * (b - 1) + p
            for x1 in (2 * x2, 2 * x2 + 1):
                if -3 <= x1 <= 6:
                    dx = -1 if x1 < 0 else (1 if x1 > 3 else 0)
                    mine = E1G[around.index((dx, 0)), x1 - 4 * dx, 0] if dx else B1[OWN1 + x1, 0:8]
                    rim = rim1(x1, 0)
                    A1[OWN1 + x1, 0:8] = mine + grown[0:8, 128 * p : 128 * p + 128]
                    A1[OWN1 + x1, 8:16] = rim + grown[8:16, 128 * p : 128 * p + 128]
    loop(1, 9, sweep1(A1, B1), 8)
    loop(2, 8, sweep1(B1, A1), 8)

    stretched = times_right(A1[2:8].reshape(96, 128), double_z())
    i, j = iotas(32, 16)
    twice = zero_one(i // 2 == j)
    for q in range(6):
        grown = times_left(twice, stretched[16 * q : 16 * q + 16])
        for p in (5 + 2 * q, 6 + 2 * q):
            EA[p] = EB[p] + grown
    loop(6, 16, sweep0(EA, EB), BY_SWEEP)

    def last(p):
        here = EB[p, 0:16]
        out[p - OWN] = (1.0 - OMEGA) * here + IV[p, 0:16] * (R0[p, 0:16] + pull_at(p, EB, *level0, keep=16))

    done = []
    for i, first in enumerate((OWN, OWN + 4)):
        loop(first, first + 4, last, BY_LAST)

    for copy in halo + tail + near + kx + e2x:
        copy.wait_send()
    remote(GK.at[0 : nn - 1], GK.at[0 : nn - 1], kz_s.at[0], kz_r.at[0], (w, n)).wait_send()
    remote(arrived, arrived, rz_s.at[0], rz_r.at[0], (w, n)).wait_send()
    remote(column, column, k3_s.at[0], k3_r.at[0], (w, n)).wait_send()
    remote(K3G.at[0:7], K3G.at[0:7], k4_s.at[0], k4_r.at[0], (w, n)).wait_send()
    from_all(R3G, r3_s, r3_r).wait_send()
    for copy in done:
        copy.wait()


def solution(mesh):
    nw, nn = mesh.shape["wide"], mesh.shape["narrow"]

    def per_device(right_side, coefficient):
        fine = pltpu.VMEM((PLANES, 32, 256), F32)
        with_zeros = pltpu.VMEM((PLANES + 8, 32, 256), F32)
        middle = pltpu.VMEM((PLANES1, 16, 128), F32)
        coarse = pltpu.VMEM((4, nw, 128), F32)
        vmem = lambda *shape: pltpu.VMEM(shape, F32)
        dma = lambda count: pltpu.SemaphoreType.DMA((count,))
        scratch = [with_zeros, with_zeros] + [fine] * 7
        scratch += [vmem(8, 32, 256), vmem(4, 3, 8, 256), vmem(4, 3, 8, 256), vmem(4, 2, 8, 256), vmem(4, 2, 8, 256)]
        scratch += [vmem(320, 128), vmem(8, 16, 256)]
        scratch += [middle] * 9 + [vmem(2, 4, 3, 8, 128), vmem(8, 4, 3, 8, 128), vmem(8, 128)]
        scratch += [vmem(2, 4, 128), vmem(3 * nn, 4, 128), vmem(4, 128), vmem(nn, 4, 128)]
        scratch += [vmem(2, 32, 128), vmem(5, 32, 128)]
        scratch += [vmem(4, 128), vmem(8, nw // 8, 4, 128), vmem(4, 128), vmem(nw, 4, 128), vmem(4 * nw, 128)]
        scratch += [coarse] * 7
        scratch += [vmem(2, 2, 32, 128), vmem(5, 2, 32, 128), vmem(4, nw + 16, 128), vmem(40, 128)]
        scratch += [dma(2), dma(8), dma(8), dma(8), dma(8), dma(1), dma(1), dma(1), dma(1), dma(4), dma(4), dma(8), dma(8)]
        scratch += [dma(1), dma(1), dma(1), dma(1), dma(1), dma(1), dma(4), dma(4)]
        return pl.pallas_call(
            functools.partial(kernel, nw, nn),
            out_shape=jax.ShapeDtypeStruct((8, 16, 256), F32),
            in_specs=[pl.BlockSpec(memory_space=pltpu.HBM)] * 2,
            out_specs=pl.BlockSpec(memory_space=pltpu.VMEM),
            scratch_shapes=scratch,
            compiler_params=pltpu.CompilerParams(
                collective_id=0, has_side_effects=True, vmem_limit_bytes=55040 * 1024
            ),
        )(right_side, coefficient)

    placed = P("wide", "narrow", None)
    return jax.shard_map(per_device, mesh=mesh, in_specs=(placed, placed), out_specs=placed, check_vma=False)
```

```python
import functools

import jax
import jax.numpy as jnp
from jax import lax
from jax.experimental import pallas as pl
from jax.experimental.pallas import tpu as pltpu
from jax.sharding import PartitionSpec as P

COARSE_ITERS = 5
OMEGA = 0.8
MESH = pl.DeviceIdType.MESH
F32 = jnp.float32

OWN = 7
PLANES = 22
HALO_K, HALO_R = 7, 6
BY_WEIGHTS, BY_FIRST, BY_SWEEP, BY_RESIDUAL, BY_LAST = 4, 10, 3, 2, 4
OWN1 = 3
PLANES1 = 10


def split(x):
    high = x.astype(jnp.bfloat16)
    rest = x - high.astype(F32)
    middle = rest.astype(jnp.bfloat16)
    low = (rest - middle.astype(F32)).astype(jnp.bfloat16)
    return high, middle, low


def times_right(x, zero_one):
    rows = x.shape[0]
    out = jnp.dot(jnp.concatenate(split(x), axis=0), zero_one, preferred_element_type=F32)
    return out[:rows] + out[rows : 2 * rows] + out[2 * rows :]


def times_left(zero_one, x):
    columns = x.shape[1]
    out = jnp.dot(zero_one, jnp.concatenate(split(x), axis=1), preferred_element_type=F32)
    return out[:, :columns] + out[:, columns : 2 * columns] + out[:, 2 * columns :]


def iotas(rows, columns):
    shape = (rows, columns)
    return lax.broadcasted_iota(jnp.int32, shape, 0), lax.broadcasted_iota(jnp.int32, shape, 1)


def zero_one(condition):
    return jnp.where(condition, 1.0, 0.0).astype(jnp.bfloat16)


def halve_z():
    fine, coarse = iotas(256, 128)
    return zero_one(fine // 2 == coarse)


def double_z():
    coarse, fine = iotas(128, 256)
    return zero_one(fine // 2 == coarse)


def reciprocal(x):
    guess = pl.reciprocal(x, approx=True)
    return guess * (2.0 - x * guess)


def weights(k, wx, wy, wz, diag, inv):
    rows, columns = k.shape[1:]
    lane = lax.broadcasted_iota(jnp.int32, (rows, columns), 1)
    rim = jnp.where((lane == 0) | (lane == columns - 1), 0.5, 0.0)
    half = jnp.where(lane == columns - 1, 0.0, 0.5)

    def plane(p):
        here = k[p]
        x = 0.5 * (here + k[p + 1])
        lower = 0.5 * (here + k[p - 1])
        y = 0.5 * (here + pltpu.roll(here, rows - 1, 0))
        z = half * (here + pltpu.roll(here, columns - 1, 1))
        d = (x + lower) + (y + pltpu.roll(y, 1, 0)) + (z + pltpu.roll(z, 1, 1)) + rim * here
        wx[p] = x
        wy[p] = y
        wz[p] = z
        diag[p] = d
        inv[p] = jnp.where(here > 0.0, OMEGA * reciprocal(d), 0.0)

    return plane


def pull_at(p, v, wx, wy, wz, keep=None):
    rows, columns = v.shape[1:]
    keep = rows if keep is None else keep
    here = v[p]
    y, z = wy[p], wz[p]
    total = wx[p, :keep] * v[p + 1, :keep] + wx[p - 1, :keep] * v[p - 1, :keep]
    total += y[:keep] * pltpu.roll(here, rows - 1, 0)[:keep] + pltpu.roll(y * here, 1, 0)[:keep]
    here, z = here[:keep], z[:keep]
    total += z * pltpu.roll(here, columns - 1, 1) + pltpu.roll(z * here, 1, 1)
    return total


def far_first(size):
    return sorted(range(1, size), key=lambda d: -min(d, size - d))


def loop(first, last, body, by):
    if last - first <= by:
        for p in range(first, last):
            body(p)
        return

    def step(i, carry):
        for p in range(by):
            body(first + i * by + p)
        return carry

    whole = (last - first) // by
    lax.fori_loop(0, whole, step, 0)
    for p in range(first + whole * by, last):
        body(p)


def turns(y_low):
    return lambda x, by: pltpu.roll(x, (by if y_low else -by) % 8, 0)


def from_corner(y_low):
    sub = lax.broadcasted_iota(jnp.int32, (8, 256), 0)
    return 7 - sub if y_low else sub


def pack_k(k, y_low):
    near, turn = from_corner(y_low), turns(y_low)
    return [
        jnp.where(near < 6, k[0], turn(k[4], 2)),
        jnp.where(near < 5, k[1], turn(k[3], 3)),
        jnp.where(near < 4, k[2], turn(k[5], 4)),
    ]


def unpack_k(tiles, y_low):
    turn = turns(y_low)
    one, two, three = tiles
    return [one, two, three, turn(two, -3), turn(one, -2), turn(three, -4)]


def pack_r(r, y_low):
    near, turn = from_corner(y_low), turns(y_low)
    return [
        jnp.where(near < 5, r[0], turn(r[2], 3)),
        jnp.where(near < 4, r[1], jnp.where(near >= 6, turn(r[3], 2), turn(r[4], 4))),
    ]


def unpack_r(tiles, y_low):
    turn = turns(y_low)
    one, two = tiles
    return [one, two, turn(one, -3), turn(two, -2), turn(two, -4)]


def kernel(nw, nn, r_in, k_in, out, *refs):
    (K0, R0, EA, EB, WX, WY, WZ, DG, IV, XS, CK, CKR, CR, CRR, T0, OUT,
     K1, R1, A1, B1, WX1, WY1, WZ1, DG1, IV1, E1S, E1G, T1,
     SB2, G2, KS, GK, K2X, K2S, K3S, K3G, R3S, R3G, F3,
     X3, Y3, Z3, D3, S3, Q3, P3, MB, E2G, E3, DS,
     load, halo_s, halo_r, tail_s, tail_r, kz_s, kz_r, rz_s, rz_r, kx_s, kx_r, e1_s, e1_r,
     k3_s, k3_r, k4_s, k4_r, r3_s, r3_r, e2_s, e2_r) = refs
    w, n = lax.axis_index("wide"), lax.axis_index("narrow")
    wide = lambda d: lax.rem(w + (d + nw), nw)
    narrow = lambda d: lax.rem(n + (d + nn), nn)

    ny = nw // 8
    in_row, in_column = lax.rem(w, 8), w // 8

    def outside(dx, dy):
        over = jnp.int32(0)
        if dx:
            over = over + jnp.where(w == (nw - 1 if dx > 0 else 0), 1, 0)
            if abs(dx) == 2:
                over = over + jnp.where(w == (nw - 2 if dx > 0 else 1), 1, 0)
        if dy:
            over = over + jnp.where(n == (nn - 1 if dy > 0 else 0), 1, 0)
        return jnp.where(over > 0, 1, 0)

    def remote(src, dst, send, recv, to):
        return pltpu.make_async_remote_copy(
            src_ref=src, dst_ref=dst, send_sem=send, recv_sem=recv, device_id=to, device_id_type=MESH
        )

    load_k = pltpu.make_async_copy(k_in, K0.at[OWN : OWN + 8, 0:16], load.at[0])
    load_r = pltpu.make_async_copy(r_in, R0.at[OWN : OWN + 8, 0:16], load.at[1])
    load_k.start()
    load_r.start()
    barrier = pltpu.get_barrier_semaphore()

    def greet(to):
        pl.semaphore_signal(barrier, inc=1, device_id=to, device_id_type=MESH)

    for dx in (-1, 1):
        for dy in (-1, 1):
            greet((wide(dx), narrow(dy)))
    ring_z, ring_y = far_first(nn), far_first(ny)
    for d in ring_z:
        greet((w, narrow(d)))
    for dx in (-1, 1):
        greet((wide(dx), n))
        greet((wide(2 * dx), n))
    for d in ring_y:
        greet((wide(8 * d), n))
    for d in range(1, 8):
        greet((8 * in_column + lax.rem(in_row + d, 8), n))
    greeted = 4 + len(ring_z) + 4 + len(ring_y) + 7

    zero_planes = jnp.zeros((8, 16, 256), F32)
    K0[PLANES : PLANES + 8, 0:16] = zero_planes
    R0[PLANES : PLANES + 8, 0:16] = zero_planes
    zero_rows = jnp.zeros((16, 256), F32)
    for p in (0, 21):
        K0[p, 16:32] = zero_rows
    for p in (1, 20):
        R0[p, 16:32] = zero_rows
    SB2[1] = jnp.zeros((4, 128), F32)
    K2X[1] = jnp.zeros((32, 128), F32)
    MB[1] = jnp.zeros((2, 32, 128), F32)
    E1S[1] = jnp.zeros((4, 3, 8, 128), F32)
    E3[...] = jnp.zeros((4, nw + 16, 128), F32)
    load_k.wait()
    load_r.wait()

    corners = [(dx, dy) for dx in (-1, 1) for dy in (-1, 1)]
    for i, (dx, dy) in enumerate(corners):
        rows = pl.ds(8, 8) if dy > 0 else pl.ds(0, 8)
        at = lambda a: OWN + (8 - a if dx > 0 else a - 1)
        keep = jnp.where(outside(dx, dy) == 0, 1.0, 0.0).astype(F32)
        for t, tile in enumerate(pack_k([K0[at(a), rows] for a in range(1, 7)], dy > 0)):
            CK[i, t] = tile * keep
        for t, tile in enumerate(pack_r([R0[at(a), rows] for a in range(1, 6)], dy > 0)):
            CR[i, t] = tile * keep

    fine, coarse = iotas(512, 128)
    to_quarter = zero_one(((fine // 256) == (coarse // 64)) & ((fine % 256) // 4 == coarse % 64))
    parts = [
        (K0[OWN + 4 * p, 0:16] + K0[OWN + 4 * p + 1, 0:16]) + (K0[OWN + 4 * p + 2, 0:16] + K0[OWN + 4 * p + 3, 0:16])
        for p in (0, 1)
    ]
    T0[0:16] = times_right(jnp.concatenate(parts, axis=1), to_quarter)
    quarter = (T0[pl.ds(0, 4, stride=4)] + T0[pl.ds(1, 4, stride=4)]) + (
        T0[pl.ds(2, 4, stride=4)] + T0[pl.ds(3, 4, stride=4)]
    )
    KS[...] = quarter * (1.0 / 64.0)

    pl.semaphore_wait(barrier, greeted)

    def send_halo(ref, width, packed, landing, send, recv):
        copies = []

        def push(src, dst, to):
            i = len(copies)
            copies.append(remote(src, dst, send.at[i], recv.at[i], to))
            copies[-1].start()

        for dy in (-1, 1):
            start = jnp.where(outside(0, dy) == 1, PLANES, OWN)
            rows = slice(8, 16) if dy > 0 else slice(0, 8)
            land = slice(24, 32) if dy > 0 else slice(16, 24)
            push(ref.at[pl.ds(start, 8), rows], ref.at[OWN : OWN + 8, land], (w, narrow(dy)))
        for dx in (-1, 1):
            start = OWN + 8 - width if dx > 0 else OWN
            land = OWN - width if dx > 0 else OWN + 8
            start = jnp.where(outside(dx, 0) == 1, PLANES, start)
            push(ref.at[pl.ds(start, width), 0:16], ref.at[land : land + width, 0:16], (wide(dx), n))
        for i, (dx, dy) in enumerate(corners):
            push(packed.at[i], landing.at[3 - i], (wide(dx), narrow(dy)))
        return copies

    def place_corners(ref, landing, unpack, count):
        for i, (dx, dy) in enumerate(corners):
            tiles = unpack([landing[i, t] for t in range(count)], dy < 0)
            rows = pl.ds(24, 8) if dy < 0 else pl.ds(16, 8)
            for a, tile in enumerate(tiles, 1):
                ref[OWN - a if dx < 0 else OWN + 7 + a, rows] = tile

    for d in far_first(nn):
        remote(KS, GK.at[n], kz_s.at[0], kz_r.at[0], (w, narrow(d))).start()
    GK[n] = KS[...]

    halo = send_halo(K0, HALO_K, CK, CKR, halo_s, halo_r)
    tail = send_halo(R0, HALO_R, CR, CRR, tail_s, tail_r)

    remote(GK.at[0 : nn - 1], GK.at[0 : nn - 1], kz_s.at[0], kz_r.at[0], (w, n)).wait_recv()
    for i in range(nn):
        K2X[0, 4 * i : 4 * i + 4] = GK[i]
    slab_k = K2X[0]
    beside = (-2, -1, 1, 2)
    kx = []
    for i, dx in enumerate(beside):
        copy = remote(K2X.at[outside(dx, 0)], K2S.at[2 - dx], kx_s.at[i], kx_r.at[i], (wide(dx), n))
        copy.start()
        kx.append(copy)
    K2S[2] = slab_k

    row, lane = iotas(32, 128)
    own_chunk = (row // 8) == (lane // 32)
    fine, coarse = iotas(128, 128)
    fold = zero_one((fine % 64) // 2 == coarse % 32)
    unfold = zero_one((coarse % 64) // 2 == fine % 32)

    def to_level3(x):
        spread = jnp.where(own_chunk, times_right(x, fold), 0.0)
        T1[...] = (spread[0:8] + spread[8:16]) + (spread[16:24] + spread[24:32])
        return T1[pl.ds(0, 4, stride=2)] + T1[pl.ds(1, 4, stride=2)]

    K3S[...] = 0.125 * to_level3(slab_k)

    for d in far_first(ny):
        remote(K3S, K3G.at[in_row, in_column], k3_s.at[0], k3_r.at[0], (wide(8 * d), n)).start()
    K3G[in_row, in_column] = K3S[...]

    for copy in halo:
        copy.wait_recv()
    place_corners(K0, CKR, unpack_k, 3)
    WX[0] = 0.5 * (K0[0] + K0[1])
    loop(1, 21, weights(K0, WX, WY, WZ, DG, IV), BY_WEIGHTS)

    for copy in tail:
        copy.wait_recv()
    place_corners(R0, CRR, unpack_r, 2)

    level0 = (WX, WY, WZ)

    def first0(p):
        EA[p] = IV[p] * R0[p]

    loop(1, 21, first0, BY_FIRST)

    def sweep0(source, target):
        def plane(p):
            target[p] = (1.0 - OMEGA) * source[p] + IV[p] * (R0[p] + pull_at(p, source, *level0))

        return plane

    loop(2, 20, sweep0(EA, EB), BY_SWEEP)

    def residual0(i):
        p = 2 * i + 3
        one, two = ((R0[q] - DG[q] * EB[q]) + pull_at(q, EB, *level0) for q in (p, p + 1))
        XS[i] = one + two

    loop(0, 8, residual0, BY_RESIDUAL)
    column = K3G.at[0, 0 : ny - 1]
    remote(column, column, k3_s.at[0], k3_r.at[0], (w, n)).wait_recv()

    def along_row(d, carry):
        to = 8 * in_column + lax.rem(in_row + d, 8)
        remote(K3G.at[in_row], K3G.at[in_row], k4_s.at[0], k4_r.at[0], (to, n)).start()
        return carry

    lax.fori_loop(1, 8, along_row, 0)

    halve = halve_z()
    T0[0:256] = times_right(XS[...].reshape(256, 256), halve)
    R1[1:9] = (0.5 * (T0[pl.ds(0, 128, stride=2)] + T0[pl.ds(1, 128, stride=2)])).reshape(8, 16, 128)
    k_pairs = jnp.concatenate([K0[2 * q + 1] + K0[2 * q + 2] for q in range(PLANES1)], axis=0)
    T0[...] = times_right(k_pairs, halve)
    K1[...] = (0.125 * (T0[pl.ds(0, 160, stride=2)] + T0[pl.ds(1, 160, stride=2)])).reshape(PLANES1, 16, 128)

    level1 = (WX1, WY1, WZ1)
    set_weights1 = weights(K1, WX1, WY1, WZ1, DG1, IV1)

    def sweep1(source, target):
        def plane(q):
            target[q] = (1.0 - OMEGA) * source[q] + IV1[q] * (R1[q] + pull_at(q, source, *level1))

        return plane

    WX1[0] = 0.5 * (K1[0] + K1[1])
    for q in range(1, 9):
        set_weights1(q)
        A1[q] = IV1[q] * R1[q]
    loop(2, 8, sweep1(A1, B1), 8)
    left = [(R1[q] - DG1[q] * B1[q]) + pull_at(q, B1, *level1) for q in range(OWN1, OWN1 + 4)]
    fine, coarse = iotas(256, 128)
    halve_pair = zero_one(((fine // 128) == (coarse // 64)) & ((fine % 128) // 2 == coarse % 64))
    pair = jnp.concatenate([(left[0] + left[1])[0:8], (left[2] + left[3])[0:8]], axis=1)
    pair = jnp.concatenate([pair, pair], axis=0)
    T0[0:16] = times_right(pair, halve_pair)
    SB2[0] = 0.5 * (T0[pl.ds(0, 4, stride=2)] + T0[pl.ds(1, 4, stride=2)])

    for copy in kx:
        copy.wait_recv()
    for d in far_first(nn) + [0]:
        for dx in (-1, 1, 0) if d else (-1, 1):
            src = SB2.at[outside(dx, 0)]
            remote(src, G2.at[(1 - dx) * nn + n], rz_s.at[0], rz_r.at[0], (wide(dx), narrow(d))).start()
    G2[nn + n] = SB2[0]

    for x1 in range(4):
        E1S[0, x1, 0] = B1[OWN1 + x1, 0:8]
        E1S[0, x1, 1] = R1[OWN1 + x1, 0:8]
        E1S[0, x1, 2] = K1[OWN1 + x1, 0:8]
    around = [(dx, dy) for dx in (-1, 0, 1) for dy in (-1, 0, 1) if dx or dy]
    near = []
    for i, (dx, dy) in enumerate(around):
        src, dst = E1S.at[outside(dx, dy)], E1G.at[7 - i]
        planes = slice(1, 4) if dx > 0 else (slice(0, 3) if dx < 0 else slice(0, 4))
        arrays = slice(0, 3) if dx and dy else slice(0, 1)
        src, dst = src.at[planes, arrays], dst.at[planes, arrays]
        copy = remote(src, dst, e1_s.at[i], e1_r.at[i], (wide(dx), narrow(dy)))
        copy.start()
        near.append(copy)

    def to_all(src, dst, send, recv):
        def one(to):
            remote(src, dst.at[w], send.at[0], recv.at[0], (to, n)).start()

        def column_of(y, d):
            return 8 * lax.rem(in_column + y, ny) + lax.rem(in_row + d, 8)

        for y in far_first(ny):
            for d in (4, 5, 3, 2, 6, 7, 1, 0):
                one(column_of(y, d))
        for d in (4, 5, 3, 2, 6, 7, 1):
            one(column_of(0, d))
        dst[w] = src[...]

    def from_all(dst, send, recv):
        return remote(dst.at[0 : nw - 1], dst.at[0 : nw - 1], send.at[0], recv.at[0], (w, n))

    k2 = K2S[...]
    row = lax.broadcasted_iota(jnp.int32, (5, 32, 128), 1)
    cell = lax.broadcasted_iota(jnp.int32, (5, 32, 128), 2)
    odd = cell >= 64
    cell = cell % 64
    none = jnp.zeros((1, 32, 128), F32)

    def above(v):
        turned = pltpu.roll(v, 64, 2)
        after = jnp.concatenate([turned[1:], none], axis=0)
        return jnp.where(odd[: v.shape[0]], after, turned)

    def below(v):
        turned = pltpu.roll(v, 64, 2)
        before = jnp.concatenate([none, turned[:-1]], axis=0)
        return jnp.where(odd[: v.shape[0]], turned, before)

    wx2 = 0.5 * (k2 + above(k2))
    wy2 = jnp.where(row == 31, 0.0, 0.5 * (k2 + pltpu.roll(k2, 31, 1)))
    wz2 = jnp.where(cell == 63, 0.0, 0.5 * (k2 + pltpu.roll(k2, 127, 2)))
    diag2 = (wx2 + below(wx2)) + (wy2 + pltpu.roll(wy2, 1, 1)) + (wz2 + pltpu.roll(wz2, 1, 2))
    diag2 += jnp.where((row == 0) | (row == 31), 0.5 * k2, 0.0) + jnp.where((cell == 0) | (cell == 63), 0.5 * k2, 0.0)
    inv2 = jnp.where(k2 > 0.0, OMEGA / diag2, 0.0)

    def image2(v, at):
        x, y, z = wx2[at], wy2[at], wz2[at]
        total = x * above(v) + below(x * v)
        total += y * pltpu.roll(v, 31, 1) + pltpu.roll(y * v, 1, 1)
        total += z * pltpu.roll(v, 127, 2) + pltpu.roll(z * v, 1, 2)
        return diag2[at] * v - total

    some = slice(1, 4)
    arrived = G2.at[0 : 3 * nn - 1]
    remote(arrived, arrived, rz_s.at[0], rz_r.at[0], (w, n)).wait_recv()
    r2 = jnp.concatenate(
        [jnp.concatenate([G2[b * nn + i] for i in range(nn)], axis=0)[None] for b in range(3)], axis=0
    )
    e2 = inv2[some] * r2
    e2 = e2 + inv2[some] * (r2 - image2(e2, some))
    left2 = (r2 - image2(e2, some))[1]
    R3S[...] = 0.5 * to_level3(left2)
    remote(K3G.at[0:7], K3G.at[0:7], k4_s.at[0], k4_r.at[0], (w, n)).wait_recv()
    to_all(R3S, R3G, r3_s, r3_r)

    MB[0, 0] = e2[1]
    MB[0, 1] = r2[1]
    e2x = []
    for i, dx in enumerate(beside):
        copy = remote(MB.at[outside(dx, 0)], E2G.at[2 - dx], e2_s.at[i], e2_r.at[i], (wide(dx), n))
        copy.start()
        e2x.append(copy)
    E2G[2] = MB[0]

    for copy in near:
        copy.wait_recv()
    sub = lax.broadcasted_iota(jnp.int32, (8, 128), 0)

    def rim1(x1, which):
        dx = -1 if x1 < 0 else (1 if x1 > 3 else 0)
        after, before = around.index((dx, 1)), around.index((dx, -1))
        return jnp.where(sub < 4, E1G[after, x1 - 4 * dx, which], E1G[before, x1 - 4 * dx, which])

    for x1 in (-3, -2, -1, 4, 5, 6):
        K1[OWN1 + x1, 8:16] = rim1(x1, 2)
        if -2 <= x1 <= 5:
            R1[OWN1 + x1, 8:16] = rim1(x1, 1)
    WX1[0] = 0.5 * (K1[0] + K1[1])
    loop(1, 9, set_weights1, 8)


    def in_order(gathered, target):
        for i in range(nw):
            F3[4 * i : 4 * i + 4] = gathered(i)
        for j in range(4):
            target[j] = F3[pl.ds(j, nw, stride=4)]

    in_order(lambda i: K3G[i % 8, i // 8], P3)
    row, lane = iotas(nw, 128)
    last_chunk, first_chunk = lane >= 96, lane < 32
    for j in range(4):
        here = P3[j]
        X3[j] = jnp.where(row == nw - 1, 0.0, 0.5 * (here + pltpu.roll(here, nw - 1, 0)))
        Z3[j] = jnp.where(lane % 32 == 31, 0.0, 0.5 * (here + pltpu.roll(here, 127, 1)))
        if j < 3:
            Y3[j] = 0.5 * (here + P3[j + 1])
        else:
            Y3[j] = jnp.where(last_chunk, 0.0, 0.5 * (here + pltpu.roll(P3[0], 96, 1)))
    for j in range(4):
        here = P3[j]
        lower = Y3[j - 1] if j else pltpu.roll(Y3[3], 32, 1)
        d = (X3[j] + pltpu.roll(X3[j], 1, 0)) + (Y3[j] + lower) + (Z3[j] + pltpu.roll(Z3[j], 1, 1))
        rim = jnp.where((row == 0) | (row == nw - 1), 0.5, 0.0)
        rim += jnp.where((lane % 32 == 0) | (lane % 32 == 31), 0.5, 0.0)
        if j == 0:
            rim += jnp.where(first_chunk, 0.5, 0.0)
        if j == 3:
            rim += jnp.where(last_chunk, 0.5, 0.0)
        D3[j] = d + rim * here

    from_all(R3G, r3_s, r3_r).wait_recv()
    in_order(lambda i: R3G[i], Q3)
    norm = jnp.zeros((nw, 128), F32)
    for j in range(4):
        P3[j] = Q3[j]
        norm += Q3[j] * Q3[j]
    norm = jnp.sum(norm, keepdims=True)

    for step in range(COARSE_ITERS):
        images = []
        dot = jnp.zeros((nw, 128), F32)
        carried = pltpu.roll(Y3[3] * P3[3], 32, 1)
        for j in range(4):
            v = P3[j]
            x, y, z = X3[j], Y3[j], Z3[j]
            total = x * pltpu.roll(v, nw - 1, 0) + pltpu.roll(x * v, 1, 0)
            total += z * pltpu.roll(v, 127, 1) + pltpu.roll(z * v, 1, 1)
            total += y * (P3[j + 1] if j < 3 else pltpu.roll(P3[0], 96, 1)) + carried
            carried = y * v
            image = D3[j] * v - total
            images.append(image)
            dot += v * image
        alpha = norm / jnp.sum(dot, keepdims=True)
        if step == COARSE_ITERS - 1:
            for j in range(4):
                S3[j] = S3[j] + alpha * P3[j]
            break
        following = jnp.zeros((nw, 128), F32)
        for j in range(4):
            rest = Q3[j] - alpha * images[j]
            Q3[j] = rest
            following += rest * rest
        following = jnp.sum(following, keepdims=True)
        beta = following / norm
        for j in range(4):
            S3[j] = (S3[j] + alpha * P3[j]) if step else alpha * P3[j]
            P3[j] = Q3[j] + beta * P3[j]
        norm = following
    for j in range(4):
        E3[j, 8 : 8 + nw] = S3[j]

    for i in range(5):
        for j in range(4):
            DS[8 * i + 2 * j : 8 * i + 2 * j + 2] = jnp.broadcast_to(E3[j, pl.ds(w + (6 + i), 1)], (2, 128))
    chunk = lax.broadcasted_iota(jnp.int32, (8, 128), 1) // 32
    rows = [jnp.where(chunk == c, DS[8 * i : 8 * i + 8], 0.0) for i in range(5) for c in range(4)]
    added = times_right(jnp.concatenate(rows, axis=0), unfold).reshape(5, 32, 128)
    for copy in e2x:
        copy.wait_recv()
    r2 = E2G[:, 1]
    e2 = E2G[:, 0] + added
    every = slice(0, 5)
    e2 = e2 + inv2 * (r2 - image2(e2, every))
    e2 = e2 + inv2 * (r2 - image2(e2, every))

    coarse, fine = iotas(128, 256)
    double_pair = zero_one(((fine // 128) == (coarse // 64)) & ((fine % 128) // 2 == coarse % 64))
    stretched = times_right(e2[1:4].reshape(96, 128), double_pair)
    i, y2 = iotas(16, 32)
    y1 = 8 * n + jnp.where(i < 12, i, i - 16)
    pick = zero_one((y1 == 2 * y2) | (y1 == 2 * y2 + 1))
    for b in range(3):
        grown = times_left(pick, stretched[32 * b : 32 * b + 32])
        for p in range(2):
            x2 = 2 * (b - 1) + p
            for x1 in (2 * x2, 2 * x2 + 1):
                if -3 <= x1 <= 6:
                    dx = -1 if x1 < 0 else (1 if x1 > 3 else 0)
                    mine = E1G[around.index((dx, 0)), x1 - 4 * dx, 0] if dx else B1[OWN1 + x1, 0:8]
                    rim = rim1(x1, 0)
                    A1[OWN1 + x1, 0:8] = mine + grown[0:8, 128 * p : 128 * p + 128]
                    A1[OWN1 + x1, 8:16] = rim + grown[8:16, 128 * p : 128 * p + 128]
    loop(1, 9, sweep1(A1, B1), 8)
    loop(2, 8, sweep1(B1, A1), 8)

    stretched = times_right(A1[2:8].reshape(96, 128), double_z())
    i, j = iotas(32, 16)
    twice = zero_one(i // 2 == j)
    for q in range(6):
        grown = times_left(twice, stretched[16 * q : 16 * q + 16])
        for p in (5 + 2 * q, 6 + 2 * q):
            EA[p] = EB[p] + grown
    loop(6, 16, sweep0(EA, EB), BY_SWEEP)

    def last(p):
        here = EB[p, 0:16]
        out[p - OWN] = (1.0 - OMEGA) * here + IV[p, 0:16] * (R0[p, 0:16] + pull_at(p, EB, *level0, keep=16))

    done = []
    for i, first in enumerate((OWN, OWN + 4)):
        loop(first, first + 4, last, BY_LAST)

    for copy in halo + tail + near + kx + e2x:
        copy.wait_send()
    remote(GK.at[0 : nn - 1], GK.at[0 : nn - 1], kz_s.at[0], kz_r.at[0], (w, n)).wait_send()
    remote(arrived, arrived, rz_s.at[0], rz_r.at[0], (w, n)).wait_send()
    remote(column, column, k3_s.at[0], k3_r.at[0], (w, n)).wait_send()
    remote(K3G.at[0:7], K3G.at[0:7], k4_s.at[0], k4_r.at[0], (w, n)).wait_send()
    from_all(R3G, r3_s, r3_r).wait_send()
    for copy in done:
        copy.wait()


def solution(mesh):
    nw, nn = mesh.shape["wide"], mesh.shape["narrow"]

    def per_device(right_side, coefficient):
        fine = pltpu.VMEM((PLANES, 32, 256), F32)
        with_zeros = pltpu.VMEM((PLANES + 8, 32, 256), F32)
        middle = pltpu.VMEM((PLANES1, 16, 128), F32)
        coarse = pltpu.VMEM((4, nw, 128), F32)
        vmem = lambda *shape: pltpu.VMEM(shape, F32)
        dma = lambda count: pltpu.SemaphoreType.DMA((count,))
        scratch = [with_zeros, with_zeros] + [fine] * 7
        scratch += [vmem(8, 32, 256), vmem(4, 3, 8, 256), vmem(4, 3, 8, 256), vmem(4, 2, 8, 256), vmem(4, 2, 8, 256)]
        scratch += [vmem(320, 128), vmem(8, 16, 256)]
        scratch += [middle] * 9 + [vmem(2, 4, 3, 8, 128), vmem(8, 4, 3, 8, 128), vmem(8, 128)]
        scratch += [vmem(2, 4, 128), vmem(3 * nn, 4, 128), vmem(4, 128), vmem(nn, 4, 128)]
        scratch += [vmem(2, 32, 128), vmem(5, 32, 128)]
        scratch += [vmem(4, 128), vmem(8, nw // 8, 4, 128), vmem(4, 128), vmem(nw, 4, 128), vmem(4 * nw, 128)]
        scratch += [coarse] * 7
        scratch += [vmem(2, 2, 32, 128), vmem(5, 2, 32, 128), vmem(4, nw + 16, 128), vmem(40, 128)]
        scratch += [dma(2), dma(8), dma(8), dma(8), dma(8), dma(1), dma(1), dma(1), dma(1), dma(4), dma(4), dma(8), dma(8)]
        scratch += [dma(1), dma(1), dma(1), dma(1), dma(1), dma(1), dma(4), dma(4)]
        return pl.pallas_call(
            functools.partial(kernel, nw, nn),
            out_shape=jax.ShapeDtypeStruct((8, 16, 256), F32),
            in_specs=[pl.BlockSpec(memory_space=pltpu.HBM)] * 2,
            out_specs=pl.BlockSpec(memory_space=pltpu.VMEM),
            scratch_shapes=scratch,
            compiler_params=pltpu.CompilerParams(
                collective_id=0, has_side_effects=True, vmem_limit_bytes=55040 * 1024
            ),
        )(right_side, coefficient)

    placed = P("wide", "narrow")
    return jax.shard_map(per_device, mesh=mesh, in_specs=(placed, placed), out_specs=placed, check_vma=False)
```

```python
import functools

import jax
import jax.numpy as jnp
from jax import lax
from jax.experimental import pallas as pl
from jax.experimental.pallas import tpu as pltpu
from jax.sharding import PartitionSpec as P

COARSE_ITERS = 5
OMEGA = 0.8
MESH = pl.DeviceIdType.MESH
F32 = jnp.float32

OWN = 7
PLANES = 22
HALO_K, HALO_R = 7, 6
BY_WEIGHTS, BY_FIRST, BY_SWEEP, BY_RESIDUAL, BY_LAST = 5, 20, 9, 8, 4
OWN1 = 3
PLANES1 = 10


def split(x):
    high = x.astype(jnp.bfloat16)
    rest = x - high.astype(F32)
    middle = rest.astype(jnp.bfloat16)
    low = (rest - middle.astype(F32)).astype(jnp.bfloat16)
    return high, middle, low


def times_right(x, zero_one):
    rows = x.shape[0]
    out = jnp.dot(jnp.concatenate(split(x), axis=0), zero_one, preferred_element_type=F32)
    return out[:rows] + out[rows : 2 * rows] + out[2 * rows :]


def times_left(zero_one, x):
    columns = x.shape[1]
    out = jnp.dot(zero_one, jnp.concatenate(split(x), axis=1), preferred_element_type=F32)
    return out[:, :columns] + out[:, columns : 2 * columns] + out[:, 2 * columns :]


def iotas(rows, columns):
    shape = (rows, columns)
    return lax.broadcasted_iota(jnp.int32, shape, 0), lax.broadcasted_iota(jnp.int32, shape, 1)


def zero_one(condition):
    return jnp.where(condition, 1.0, 0.0).astype(jnp.bfloat16)


def halve_z():
    fine, coarse = iotas(256, 128)
    return zero_one(fine // 2 == coarse)


def double_z():
    coarse, fine = iotas(128, 256)
    return zero_one(fine // 2 == coarse)


def reciprocal(x):
    guess = pl.reciprocal(x, approx=True)
    return guess * (2.0 - x * guess)


def weights(k, wx, wy, wz, diag, inv):
    rows, columns = k.shape[1:]
    lane = lax.broadcasted_iota(jnp.int32, (rows, columns), 1)
    rim = jnp.where((lane == 0) | (lane == columns - 1), 0.5, 0.0)
    half = jnp.where(lane == columns - 1, 0.0, 0.5)

    def plane(p):
        here = k[p]
        x = 0.5 * (here + k[p + 1])
        lower = 0.5 * (here + k[p - 1])
        y = 0.5 * (here + pltpu.roll(here, rows - 1, 0))
        z = half * (here + pltpu.roll(here, columns - 1, 1))
        d = (x + lower) + (y + pltpu.roll(y, 1, 0)) + (z + pltpu.roll(z, 1, 1)) + rim * here
        wx[p] = x
        wy[p] = y
        wz[p] = z
        diag[p] = d
        inv[p] = jnp.where(here > 0.0, OMEGA * reciprocal(d), 0.0)

    return plane


def pull_at(p, v, wx, wy, wz, keep=None):
    rows, columns = v.shape[1:]
    keep = rows if keep is None else keep
    here = v[p]
    y, z = wy[p], wz[p]
    total = wx[p, :keep] * v[p + 1, :keep] + wx[p - 1, :keep] * v[p - 1, :keep]
    total += y[:keep] * pltpu.roll(here, rows - 1, 0)[:keep] + pltpu.roll(y * here, 1, 0)[:keep]
    here, z = here[:keep], z[:keep]
    total += z * pltpu.roll(here, columns - 1, 1) + pltpu.roll(z * here, 1, 1)
    return total


def far_first(size):
    return sorted(range(1, size), key=lambda d: -min(d, size - d))


def loop(first, last, body, by):
    if last - first <= by:
        for p in range(first, last):
            body(p)
        return

    def step(i, carry):
        for p in range(by):
            body(first + i * by + p)
        return carry

    whole = (last - first) // by
    lax.fori_loop(0, whole, step, 0)
    for p in range(first + whole * by, last):
        body(p)


def turns(y_low):
    return lambda x, by: pltpu.roll(x, (by if y_low else -by) % 8, 0)


def from_corner(y_low):
    sub = lax.broadcasted_iota(jnp.int32, (8, 256), 0)
    return 7 - sub if y_low else sub


def pack_k(k, y_low):
    near, turn = from_corner(y_low), turns(y_low)
    return [
        jnp.where(near < 6, k[0], turn(k[4], 2)),
        jnp.where(near < 5, k[1], turn(k[3], 3)),
        jnp.where(near < 4, k[2], turn(k[5], 4)),
    ]


def unpack_k(tiles, y_low):
    turn = turns(y_low)
    one, two, three = tiles
    return [one, two, three, turn(two, -3), turn(one, -2), turn(three, -4)]


def pack_r(r, y_low):
    near, turn = from_corner(y_low), turns(y_low)
    return [
        jnp.where(near < 5, r[0], turn(r[2], 3)),
        jnp.where(near < 4, r[1], jnp.where(near >= 6, turn(r[3], 2), turn(r[4], 4))),
    ]


def unpack_r(tiles, y_low):
    turn = turns(y_low)
    one, two = tiles
    return [one, two, turn(one, -3), turn(two, -2), turn(two, -4)]


def kernel(nw, nn, r_in, k_in, out, *refs):
    (K0, R0, EA, EB, WX, WY, WZ, DG, IV, XS, CK, CKR, CR, CRR, T0, OUT,
     K1, R1, A1, B1, WX1, WY1, WZ1, DG1, IV1, E1S, E1G, T1,
     SB2, G2, KS, GK, K2X, K2S, K3S, K3G, R3S, R3G, F3,
     X3, Y3, Z3, D3, S3, Q3, P3, A3, MB, E2G, E3, DS,
     load, halo_s, halo_r, tail_s, tail_r, kz_s, kz_r, rz_s, rz_r, kx_s, kx_r, e1_s, e1_r,
     k3_s, k3_r, k4_s, k4_r, r3_s, r3_r, e2_s, e2_r) = refs
    w, n = lax.axis_index("wide"), lax.axis_index("narrow")
    wide = lambda d: lax.rem(w + (d + nw), nw)
    narrow = lambda d: lax.rem(n + (d + nn), nn)

    ny = nw // 8
    in_row, in_column = lax.rem(w, 8), w // 8

    def outside(dx, dy):
        over = jnp.int32(0)
        if dx:
            over = over + jnp.where(w == (nw - 1 if dx > 0 else 0), 1, 0)
            if abs(dx) == 2:
                over = over + jnp.where(w == (nw - 2 if dx > 0 else 1), 1, 0)
        if dy:
            over = over + jnp.where(n == (nn - 1 if dy > 0 else 0), 1, 0)
        return jnp.where(over > 0, 1, 0)

    def remote(src, dst, send, recv, to):
        return pltpu.make_async_remote_copy(
            src_ref=src, dst_ref=dst, send_sem=send, recv_sem=recv, device_id=to, device_id_type=MESH
        )

    load_k = pltpu.make_async_copy(k_in, K0.at[OWN : OWN + 8, 0:16], load.at[0])
    load_r = pltpu.make_async_copy(r_in, R0.at[OWN : OWN + 8, 0:16], load.at[1])
    load_k.start()
    load_r.start()
    barrier = pltpu.get_barrier_semaphore()

    def greet(to):
        pl.semaphore_signal(barrier, inc=1, device_id=to, device_id_type=MESH)

    for dx in (-1, 1):
        for dy in (-1, 1):
            greet((wide(dx), narrow(dy)))
    ring_z, ring_y = far_first(nn), far_first(ny)
    for d in ring_z:
        greet((w, narrow(d)))
    for dx in (-1, 1):
        greet((wide(dx), n))
        greet((wide(2 * dx), n))
    for d in ring_y:
        greet((wide(8 * d), n))
    for d in range(1, 8):
        greet((8 * in_column + lax.rem(in_row + d, 8), n))
    greeted = 4 + len(ring_z) + 4 + len(ring_y) + 7

    zero_planes = jnp.zeros((8, 16, 256), F32)
    K0[PLANES : PLANES + 8, 0:16] = zero_planes
    R0[PLANES : PLANES + 8, 0:16] = zero_planes
    zero_rows = jnp.zeros((16, 256), F32)
    for p in (0, 21):
        K0[p, 16:32] = zero_rows
    for p in (1, 20):
        R0[p, 16:32] = zero_rows
    SB2[1] = jnp.zeros((4, 128), F32)
    K2X[1] = jnp.zeros((32, 128), F32)
    MB[1] = jnp.zeros((2, 32, 128), F32)
    E1S[1] = jnp.zeros((4, 3, 8, 128), F32)
    E3[...] = jnp.zeros((4, 8, 16, 128), F32)
    load_k.wait()
    load_r.wait()

    corners = [(dx, dy) for dx in (-1, 1) for dy in (-1, 1)]
    for i, (dx, dy) in enumerate(corners):
        rows = pl.ds(8, 8) if dy > 0 else pl.ds(0, 8)
        at = lambda a: OWN + (8 - a if dx > 0 else a - 1)
        keep = jnp.where(outside(dx, dy) == 0, 1.0, 0.0).astype(F32)
        for t, tile in enumerate(pack_k([K0[at(a), rows] for a in range(1, 7)], dy > 0)):
            CK[i, t] = tile * keep
        for t, tile in enumerate(pack_r([R0[at(a), rows] for a in range(1, 6)], dy > 0)):
            CR[i, t] = tile * keep

    fine, coarse = iotas(512, 128)
    to_quarter = zero_one(((fine // 256) == (coarse // 64)) & ((fine % 256) // 4 == coarse % 64))
    parts = [
        (K0[OWN + 4 * p, 0:16] + K0[OWN + 4 * p + 1, 0:16]) + (K0[OWN + 4 * p + 2, 0:16] + K0[OWN + 4 * p + 3, 0:16])
        for p in (0, 1)
    ]
    T0[0:16] = times_right(jnp.concatenate(parts, axis=1), to_quarter)
    quarter = (T0[pl.ds(0, 4, stride=4)] + T0[pl.ds(1, 4, stride=4)]) + (
        T0[pl.ds(2, 4, stride=4)] + T0[pl.ds(3, 4, stride=4)]
    )
    KS[...] = quarter * (1.0 / 64.0)

    pl.semaphore_wait(barrier, greeted)

    def send_halo(ref, width, packed, landing, send, recv):
        copies = []

        def push(src, dst, to):
            i = len(copies)
            copies.append(remote(src, dst, send.at[i], recv.at[i], to))
            copies[-1].start()

        for dy in (-1, 1):
            start = jnp.where(outside(0, dy) == 1, PLANES, OWN)
            rows = slice(8, 16) if dy > 0 else slice(0, 8)
            land = slice(24, 32) if dy > 0 else slice(16, 24)
            push(ref.at[pl.ds(start, 8), rows], ref.at[OWN : OWN + 8, land], (w, narrow(dy)))
        for dx in (-1, 1):
            start = OWN + 8 - width if dx > 0 else OWN
            land = OWN - width if dx > 0 else OWN + 8
            start = jnp.where(outside(dx, 0) == 1, PLANES, start)
            push(ref.at[pl.ds(start, width), 0:16], ref.at[land : land + width, 0:16], (wide(dx), n))
        for i, (dx, dy) in enumerate(corners):
            push(packed.at[i], landing.at[3 - i], (wide(dx), narrow(dy)))
        return copies

    def place_corners(ref, landing, unpack, count):
        for i, (dx, dy) in enumerate(corners):
            tiles = unpack([landing[i, t] for t in range(count)], dy < 0)
            rows = pl.ds(24, 8) if dy < 0 else pl.ds(16, 8)
            for a, tile in enumerate(tiles, 1):
                ref[OWN - a if dx < 0 else OWN + 7 + a, rows] = tile

    for d in far_first(nn):
        remote(KS, GK.at[n], kz_s.at[0], kz_r.at[0], (w, narrow(d))).start()
    GK[n] = KS[...]

    halo = send_halo(K0, HALO_K, CK, CKR, halo_s, halo_r)
    tail = send_halo(R0, HALO_R, CR, CRR, tail_s, tail_r)

    remote(GK.at[0 : nn - 1], GK.at[0 : nn - 1], kz_s.at[0], kz_r.at[0], (w, n)).wait_recv()
    for i in range(nn):
        K2X[0, 4 * i : 4 * i + 4] = GK[i]
    slab_k = K2X[0]
    beside = (-2, -1, 1, 2)
    kx = []
    for i, dx in enumerate(beside):
        copy = remote(K2X.at[outside(dx, 0)], K2S.at[2 - dx], kx_s.at[i], kx_r.at[i], (wide(dx), n))
        copy.start()
        kx.append(copy)
    K2S[2] = slab_k

    row, lane = iotas(32, 128)
    own_chunk = (row // 8) == (lane // 32)
    fine, coarse = iotas(128, 128)
    fold = zero_one((fine % 64) // 2 == coarse % 32)
    unfold = zero_one((coarse % 64) // 2 == fine % 32)

    def to_level3(x):
        spread = jnp.where(own_chunk, times_right(x, fold), 0.0)
        T1[...] = (spread[0:8] + spread[8:16]) + (spread[16:24] + spread[24:32])
        return T1[pl.ds(0, 4, stride=2)] + T1[pl.ds(1, 4, stride=2)]

    K3S[...] = 0.125 * to_level3(slab_k)

    for d in far_first(ny):
        remote(K3S, K3G.at[in_row, in_column], k3_s.at[0], k3_r.at[0], (wide(8 * d), n)).start()
    K3G[in_row, in_column] = K3S[...]

    for copy in halo:
        copy.wait_recv()
    place_corners(K0, CKR, unpack_k, 3)
    WX[0] = 0.5 * (K0[0] + K0[1])
    loop(1, 21, weights(K0, WX, WY, WZ, DG, IV), BY_WEIGHTS)

    halve = halve_z()
    k_pairs = jnp.concatenate([K0[2 * q + 1] + K0[2 * q + 2] for q in range(PLANES1)], axis=0)
    T0[...] = times_right(k_pairs, halve)
    K1[...] = (0.125 * (T0[pl.ds(0, 160, stride=2)] + T0[pl.ds(1, 160, stride=2)])).reshape(PLANES1, 16, 128)
    level1 = (WX1, WY1, WZ1)
    set_weights1 = weights(K1, WX1, WY1, WZ1, DG1, IV1)
    WX1[0] = 0.5 * (K1[0] + K1[1])
    loop(1, 9, set_weights1, 8)

    for copy in tail:
        copy.wait_recv()
    place_corners(R0, CRR, unpack_r, 2)

    level0 = (WX, WY, WZ)

    def first0(p):
        EA[p] = IV[p] * R0[p]

    loop(1, 21, first0, BY_FIRST)

    def sweep0(source, target):
        def plane(p):
            target[p] = (1.0 - OMEGA) * source[p] + IV[p] * (R0[p] + pull_at(p, source, *level0))

        return plane

    loop(2, 20, sweep0(EA, EB), BY_SWEEP)

    def residual0(i):
        p = 2 * i + 3
        one, two = ((R0[q] - DG[q] * EB[q]) + pull_at(q, EB, *level0) for q in (p, p + 1))
        XS[i] = one + two

    loop(0, 8, residual0, BY_RESIDUAL)
    column = K3G.at[0, 0 : ny - 1]
    remote(column, column, k3_s.at[0], k3_r.at[0], (w, n)).wait_recv()

    def along_row(d, carry):
        to = 8 * in_column + lax.rem(in_row + d, 8)
        remote(K3G.at[in_row], K3G.at[in_row], k4_s.at[0], k4_r.at[0], (to, n)).start()
        return carry

    lax.fori_loop(1, 8, along_row, 0)

    T0[0:256] = times_right(XS[...].reshape(256, 256), halve)
    R1[1:9] = (0.5 * (T0[pl.ds(0, 128, stride=2)] + T0[pl.ds(1, 128, stride=2)])).reshape(8, 16, 128)
    def sweep1(source, target):
        def plane(q):
            target[q] = (1.0 - OMEGA) * source[q] + IV1[q] * (R1[q] + pull_at(q, source, *level1))

        return plane

    for q in range(1, 9):
        A1[q] = IV1[q] * R1[q]
    loop(2, 8, sweep1(A1, B1), 8)
    left = [(R1[q] - DG1[q] * B1[q]) + pull_at(q, B1, *level1) for q in range(OWN1, OWN1 + 4)]
    fine, coarse = iotas(256, 128)
    halve_pair = zero_one(((fine // 128) == (coarse // 64)) & ((fine % 128) // 2 == coarse % 64))
    pair = jnp.concatenate([(left[0] + left[1])[0:8], (left[2] + left[3])[0:8]], axis=1)
    pair = jnp.concatenate([pair, pair], axis=0)
    T0[0:16] = times_right(pair, halve_pair)
    SB2[0] = 0.5 * (T0[pl.ds(0, 4, stride=2)] + T0[pl.ds(1, 4, stride=2)])

    for copy in kx:
        copy.wait_recv()
    for d in far_first(nn) + [0]:
        for dx in (-1, 1, 0) if d else (-1, 1):
            src = SB2.at[outside(dx, 0)]
            remote(src, G2.at[(1 - dx) * nn + n], rz_s.at[0], rz_r.at[0], (wide(dx), narrow(d))).start()
    G2[nn + n] = SB2[0]

    for x1 in range(4):
        E1S[0, x1, 0] = B1[OWN1 + x1, 0:8]
        E1S[0, x1, 1] = R1[OWN1 + x1, 0:8]
        E1S[0, x1, 2] = K1[OWN1 + x1, 0:8]
    around = [(dx, dy) for dx in (-1, 0, 1) for dy in (-1, 0, 1) if dx or dy]
    near = []
    for i, (dx, dy) in enumerate(around):
        src, dst = E1S.at[outside(dx, dy)], E1G.at[7 - i]
        planes = slice(1, 4) if dx > 0 else (slice(0, 3) if dx < 0 else slice(0, 4))
        arrays = slice(0, 3) if dx and dy else slice(0, 1)
        src, dst = src.at[planes, arrays], dst.at[planes, arrays]
        copy = remote(src, dst, e1_s.at[i], e1_r.at[i], (wide(dx), narrow(dy)))
        copy.start()
        near.append(copy)

    def to_all(src, dst, send, recv):
        def one(to):
            remote(src, dst.at[w], send.at[0], recv.at[0], (to, n)).start()

        def column_of(y, d):
            return 8 * lax.rem(in_column + y, ny) + lax.rem(in_row + d, 8)

        for y in far_first(ny):
            for d in (4, 5, 3, 2, 6, 7, 1, 0):
                one(column_of(y, d))
        for d in (4, 5, 3, 2, 6, 7, 1):
            one(column_of(0, d))
        dst[w] = src[...]

    def from_all(dst, send, recv):
        return remote(dst.at[0 : nw - 1], dst.at[0 : nw - 1], send.at[0], recv.at[0], (w, n))

    k2 = K2S[...]
    row = lax.broadcasted_iota(jnp.int32, (5, 32, 128), 1)
    cell = lax.broadcasted_iota(jnp.int32, (5, 32, 128), 2)
    odd = cell >= 64
    cell = cell % 64
    none = jnp.zeros((1, 32, 128), F32)

    def above(v):
        turned = pltpu.roll(v, 64, 2)
        after = jnp.concatenate([turned[1:], none], axis=0)
        return jnp.where(odd[: v.shape[0]], after, turned)

    def below(v):
        turned = pltpu.roll(v, 64, 2)
        before = jnp.concatenate([none, turned[:-1]], axis=0)
        return jnp.where(odd[: v.shape[0]], turned, before)

    wx2 = 0.5 * (k2 + above(k2))
    wy2 = jnp.where(row == 31, 0.0, 0.5 * (k2 + pltpu.roll(k2, 31, 1)))
    wz2 = jnp.where(cell == 63, 0.0, 0.5 * (k2 + pltpu.roll(k2, 127, 2)))
    diag2 = (wx2 + below(wx2)) + (wy2 + pltpu.roll(wy2, 1, 1)) + (wz2 + pltpu.roll(wz2, 1, 2))
    diag2 += jnp.where((row == 0) | (row == 31), 0.5 * k2, 0.0) + jnp.where((cell == 0) | (cell == 63), 0.5 * k2, 0.0)
    inv2 = jnp.where(k2 > 0.0, OMEGA / diag2, 0.0)

    def image2(v, at):
        x, y, z = wx2[at], wy2[at], wz2[at]
        total = x * above(v) + below(x * v)
        total += y * pltpu.roll(v, 31, 1) + pltpu.roll(y * v, 1, 1)
        total += z * pltpu.roll(v, 127, 2) + pltpu.roll(z * v, 1, 2)
        return diag2[at] * v - total

    some = slice(1, 4)
    arrived = G2.at[0 : 3 * nn - 1]
    remote(arrived, arrived, rz_s.at[0], rz_r.at[0], (w, n)).wait_recv()
    r2 = jnp.concatenate(
        [jnp.concatenate([G2[b * nn + i] for i in range(nn)], axis=0)[None] for b in range(3)], axis=0
    )
    e2 = inv2[some] * r2
    e2 = e2 + inv2[some] * (r2 - image2(e2, some))
    left2 = (r2 - image2(e2, some))[1]
    R3S[...] = 0.5 * to_level3(left2)
    remote(K3G.at[0:7], K3G.at[0:7], k4_s.at[0], k4_r.at[0], (w, n)).wait_recv()
    to_all(R3S, R3G, r3_s, r3_r)

    MB[0, 0] = e2[1]
    MB[0, 1] = r2[1]
    e2x = []
    for i, dx in enumerate(beside):
        copy = remote(MB.at[outside(dx, 0)], E2G.at[2 - dx], e2_s.at[i], e2_r.at[i], (wide(dx), n))
        copy.start()
        e2x.append(copy)
    E2G[2] = MB[0]

    for copy in near:
        copy.wait_recv()
    sub = lax.broadcasted_iota(jnp.int32, (8, 128), 0)

    def rim1(x1, which):
        dx = -1 if x1 < 0 else (1 if x1 > 3 else 0)
        after, before = around.index((dx, 1)), around.index((dx, -1))
        return jnp.where(sub < 4, E1G[after, x1 - 4 * dx, which], E1G[before, x1 - 4 * dx, which])

    for x1 in (-3, -2, -1, 4, 5, 6):
        K1[OWN1 + x1, 8:16] = rim1(x1, 2)
        if -2 <= x1 <= 5:
            R1[OWN1 + x1, 8:16] = rim1(x1, 1)
    WX1[0] = 0.5 * (K1[0] + K1[1])
    loop(1, 9, set_weights1, 8)

    def in_order(gathered, target):
        for i in range(nw):
            F3[4 * i : 4 * i + 4] = gathered(i)
        for j in range(4):
            for t in range(8):
                target[j, t] = F3[pl.ds(4 * t + j, 8, stride=32)]

    def next_x(v):
        return jnp.concatenate([v[1:], pltpu.roll(v[0], 7, 0)[None]], axis=0)

    def last_x(v):
        return jnp.concatenate([pltpu.roll(v[7], 1, 0)[None], v[:7]], axis=0)

    in_order(lambda i: K3G[i % 8, i // 8], P3)
    cube = (8, 8, 128)
    tile, row, lane = (lax.broadcasted_iota(jnp.int32, cube, d) for d in range(3))
    first_x, final_x = (tile == 0) & (row == 0), (tile == 7) & (row == 7)
    last_chunk, first_chunk = lane >= 96, lane < 32
    for j in range(4):
        here = P3[j]
        X3[j] = jnp.where(final_x, 0.0, 0.5 * (here + next_x(here)))
        Z3[j] = jnp.where(lane % 32 == 31, 0.0, 0.5 * (here + pltpu.roll(here, 127, 2)))
        if j < 3:
            Y3[j] = 0.5 * (here + P3[j + 1])
        else:
            Y3[j] = jnp.where(last_chunk, 0.0, 0.5 * (here + pltpu.roll(P3[0], 96, 2)))
    for j in range(4):
        here = P3[j]
        lower = Y3[j - 1] if j else pltpu.roll(Y3[3], 32, 2)
        d = (X3[j] + last_x(X3[j])) + (Y3[j] + lower) + (Z3[j] + pltpu.roll(Z3[j], 1, 2))
        rim = jnp.where(first_x | final_x, 0.5, 0.0)
        rim += jnp.where((lane % 32 == 0) | (lane % 32 == 31), 0.5, 0.0)
        if j == 0:
            rim += jnp.where(first_chunk, 0.5, 0.0)
        if j == 3:
            rim += jnp.where(last_chunk, 0.5, 0.0)
        D3[j] = d + rim * here

    from_all(R3G, r3_s, r3_r).wait_recv()
    in_order(lambda i: R3G[i], Q3)

    def total_of(v):
        return jnp.sum(v.reshape(64, 128), keepdims=True).reshape(1, 1, 1)

    def image3(v):
        images = []
        carried = pltpu.roll(Y3[3] * v[3], 32, 2)
        for j in range(4):
            x, y, z = X3[j], Y3[j], Z3[j]
            total = x * next_x(v[j]) + last_x(x * v[j])
            total += z * pltpu.roll(v[j], 127, 2) + pltpu.roll(z * v[j], 1, 2)
            total += y * (v[j + 1] if j < 3 else pltpu.roll(v[0], 96, 2)) + carried
            carried = y * v[j]
            images.append(D3[j] * v[j] - total)
        return images

    norm = alpha = None
    for step in range(COARSE_ITERS):
        images = image3(Q3)
        one, two = jnp.zeros(cube, F32), jnp.zeros(cube, F32)
        for j in range(4):
            rest = Q3[j]
            one += rest * rest
            two += rest * images[j]
        following, pull = total_of(one), total_of(two)
        if step:
            beta = following / norm
            alpha = following / (pull - beta * (following / alpha))
        else:
            alpha = following / pull
        norm = following
        for j in range(4):
            direction = Q3[j] + beta * P3[j] if step else Q3[j]
            result = S3[j] + alpha * direction if step else alpha * direction
            if step == COARSE_ITERS - 1:
                E3[j, :, 1:9] = result
                continue
            carried = images[j] + beta * A3[j] if step else images[j]
            P3[j], A3[j], S3[j] = direction, carried, result
            Q3[j] = Q3[j] - alpha * carried

    for i in range(5):
        x = w + (6 + i)
        for j in range(4):
            value = E3[j, lax.rem(x, 8), pl.ds(x // 8, 1)]
            DS[8 * i + 2 * j : 8 * i + 2 * j + 2] = jnp.broadcast_to(value, (2, 128))
    chunk = lax.broadcasted_iota(jnp.int32, (8, 128), 1) // 32
    rows = [jnp.where(chunk == c, DS[8 * i : 8 * i + 8], 0.0) for i in range(5) for c in range(4)]
    added = times_right(jnp.concatenate(rows, axis=0), unfold).reshape(5, 32, 128)
    for copy in e2x:
        copy.wait_recv()
    r2 = E2G[:, 1]
    e2 = E2G[:, 0] + added
    every = slice(0, 5)
    e2 = e2 + inv2 * (r2 - image2(e2, every))
    e2 = e2 + inv2 * (r2 - image2(e2, every))

    coarse, fine = iotas(128, 256)
    double_pair = zero_one(((fine // 128) == (coarse // 64)) & ((fine % 128) // 2 == coarse % 64))
    stretched = times_right(e2[1:4].reshape(96, 128), double_pair)
    i, y2 = iotas(16, 32)
    y1 = 8 * n + jnp.where(i < 12, i, i - 16)
    pick = zero_one((y1 == 2 * y2) | (y1 == 2 * y2 + 1))
    for b in range(3):
        grown = times_left(pick, stretched[32 * b : 32 * b + 32])
        for p in range(2):
            x2 = 2 * (b - 1) + p
            for x1 in (2 * x2, 2 * x2 + 1):
                if -3 <= x1 <= 6:
                    dx = -1 if x1 < 0 else (1 if x1 > 3 else 0)
                    mine = E1G[around.index((dx, 0)), x1 - 4 * dx, 0] if dx else B1[OWN1 + x1, 0:8]
                    rim = rim1(x1, 0)
                    A1[OWN1 + x1, 0:8] = mine + grown[0:8, 128 * p : 128 * p + 128]
                    A1[OWN1 + x1, 8:16] = rim + grown[8:16, 128 * p : 128 * p + 128]
    loop(1, 9, sweep1(A1, B1), 8)
    loop(2, 8, sweep1(B1, A1), 8)

    stretched = times_right(A1[2:8].reshape(96, 128), double_z())
    i, j = iotas(32, 16)
    twice = zero_one(i // 2 == j)
    for q in range(6):
        grown = times_left(twice, stretched[16 * q : 16 * q + 16])
        for p in (5 + 2 * q, 6 + 2 * q):
            EA[p] = EB[p] + grown
    loop(6, 16, sweep0(EA, EB), BY_SWEEP)

    def last(p):
        here = EB[p, 0:16]
        out[p - OWN] = (1.0 - OMEGA) * here + IV[p, 0:16] * (R0[p, 0:16] + pull_at(p, EB, *level0, keep=16))

    done = []
    for i, first in enumerate((OWN, OWN + 4)):
        loop(first, first + 4, last, BY_LAST)

    for copy in halo + tail + near + kx + e2x:
        copy.wait_send()
    remote(GK.at[0 : nn - 1], GK.at[0 : nn - 1], kz_s.at[0], kz_r.at[0], (w, n)).wait_send()
    remote(arrived, arrived, rz_s.at[0], rz_r.at[0], (w, n)).wait_send()
    remote(column, column, k3_s.at[0], k3_r.at[0], (w, n)).wait_send()
    remote(K3G.at[0:7], K3G.at[0:7], k4_s.at[0], k4_r.at[0], (w, n)).wait_send()
    from_all(R3G, r3_s, r3_r).wait_send()
    for copy in done:
        copy.wait()


def solution(mesh):
    nw, nn = mesh.shape["wide"], mesh.shape["narrow"]

    def per_device(right_side, coefficient):
        fine = pltpu.VMEM((PLANES, 32, 256), F32)
        with_zeros = pltpu.VMEM((PLANES + 8, 32, 256), F32)
        middle = pltpu.VMEM((PLANES1, 16, 128), F32)
        coarse = pltpu.VMEM((4, 8, 8, 128), F32)
        vmem = lambda *shape: pltpu.VMEM(shape, F32)
        dma = lambda count: pltpu.SemaphoreType.DMA((count,))
        scratch = [with_zeros, with_zeros] + [fine] * 7
        scratch += [vmem(8, 32, 256), vmem(4, 3, 8, 256), vmem(4, 3, 8, 256), vmem(4, 2, 8, 256), vmem(4, 2, 8, 256)]
        scratch += [vmem(320, 128), vmem(8, 16, 256)]
        scratch += [middle] * 9 + [vmem(2, 4, 3, 8, 128), vmem(8, 4, 3, 8, 128), vmem(8, 128)]
        scratch += [vmem(2, 4, 128), vmem(3 * nn, 4, 128), vmem(4, 128), vmem(nn, 4, 128)]
        scratch += [vmem(2, 32, 128), vmem(5, 32, 128)]
        scratch += [vmem(4, 128), vmem(8, nw // 8, 4, 128), vmem(4, 128), vmem(nw, 4, 128), vmem(4 * nw, 128)]
        scratch += [coarse] * 8
        scratch += [vmem(2, 2, 32, 128), vmem(5, 2, 32, 128), vmem(4, 8, 16, 128), vmem(40, 128)]
        scratch += [dma(2), dma(8), dma(8), dma(8), dma(8), dma(1), dma(1), dma(1), dma(1), dma(4), dma(4), dma(8), dma(8)]
        scratch += [dma(1), dma(1), dma(1), dma(1), dma(1), dma(1), dma(4), dma(4)]
        return pl.pallas_call(
            functools.partial(kernel, nw, nn),
            out_shape=jax.ShapeDtypeStruct((8, 16, 256), F32),
            in_specs=[pl.BlockSpec(memory_space=pltpu.HBM)] * 2,
            out_specs=pl.BlockSpec(memory_space=pltpu.VMEM),
            scratch_shapes=scratch,
            compiler_params=pltpu.CompilerParams(
                collective_id=0, has_side_effects=True, vmem_limit_bytes=55040 * 1024
            ),
        )(right_side, coefficient)

    placed = P("wide", "narrow")
    return jax.shard_map(per_device, mesh=mesh, in_specs=(placed, placed), out_specs=placed, check_vma=False)
```

```python
import functools

import jax
import jax.numpy as jnp
from jax import lax
from jax.experimental import pallas as pl
from jax.experimental.pallas import tpu as pltpu
from jax.sharding import PartitionSpec as P

COARSE_ITERS = 5
OMEGA = 0.8
MESH = pl.DeviceIdType.MESH
F32 = jnp.float32

OWN = 7
PLANES = 22
HALO_K, HALO_R = 7, 6
BY_WEIGHTS, BY_FIRST, BY_SWEEP, BY_RESIDUAL, BY_LAST = 5, 20, 9, 8, 4
OWN1 = 3
PLANES1 = 10


def split(x):
    high = x.astype(jnp.bfloat16)
    rest = x - high.astype(F32)
    middle = rest.astype(jnp.bfloat16)
    low = (rest - middle.astype(F32)).astype(jnp.bfloat16)
    return high, middle, low


def times_right(x, zero_one):
    rows = x.shape[0]
    out = jnp.dot(jnp.concatenate(split(x), axis=0), zero_one, preferred_element_type=F32)
    return out[:rows] + out[rows : 2 * rows] + out[2 * rows :]


def times_left(zero_one, x):
    columns = x.shape[1]
    out = jnp.dot(zero_one, jnp.concatenate(split(x), axis=1), preferred_element_type=F32)
    return out[:, :columns] + out[:, columns : 2 * columns] + out[:, 2 * columns :]


def iotas(rows, columns):
    shape = (rows, columns)
    return lax.broadcasted_iota(jnp.int32, shape, 0), lax.broadcasted_iota(jnp.int32, shape, 1)


def zero_one(condition):
    return jnp.where(condition, 1.0, 0.0).astype(jnp.bfloat16)


def halve_z():
    fine, coarse = iotas(256, 128)
    return zero_one(fine // 2 == coarse)


def double_z():
    coarse, fine = iotas(128, 256)
    return zero_one(fine // 2 == coarse)


def reciprocal(x):
    guess = pl.reciprocal(x, approx=True)
    return guess * (2.0 - x * guess)


def weights(k, wx, wy, wz, diag, inv):
    rows, columns = k.shape[1:]
    lane = lax.broadcasted_iota(jnp.int32, (rows, columns), 1)
    rim = jnp.where((lane == 0) | (lane == columns - 1), 0.5, 0.0)
    half = jnp.where(lane == columns - 1, 0.0, 0.5)

    def plane(p):
        here = k[p]
        x = 0.5 * (here + k[p + 1])
        lower = 0.5 * (here + k[p - 1])
        y = 0.5 * (here + pltpu.roll(here, rows - 1, 0))
        z = half * (here + pltpu.roll(here, columns - 1, 1))
        d = (x + lower) + (y + pltpu.roll(y, 1, 0)) + (z + pltpu.roll(z, 1, 1)) + rim * here
        wx[p] = x
        wy[p] = y
        wz[p] = z
        diag[p] = d
        inv[p] = jnp.where(here > 0.0, OMEGA * reciprocal(d), 0.0)

    return plane


def pull_at(p, v, wx, wy, wz, keep=None):
    rows, columns = v.shape[1:]
    keep = rows if keep is None else keep
    here = v[p]
    y, z = wy[p], wz[p]
    total = wx[p, :keep] * v[p + 1, :keep] + wx[p - 1, :keep] * v[p - 1, :keep]
    total += y[:keep] * pltpu.roll(here, rows - 1, 0)[:keep] + pltpu.roll(y * here, 1, 0)[:keep]
    here, z = here[:keep], z[:keep]
    total += z * pltpu.roll(here, columns - 1, 1) + pltpu.roll(z * here, 1, 1)
    return total


def far_first(size):
    return sorted(range(1, size), key=lambda d: -min(d, size - d))


def loop(first, last, body, by):
    if last - first <= by:
        for p in range(first, last):
            body(p)
        return

    def step(i, carry):
        for p in range(by):
            body(first + i * by + p)
        return carry

    whole = (last - first) // by
    lax.fori_loop(0, whole, step, 0)
    for p in range(first + whole * by, last):
        body(p)


def turns(y_low):
    return lambda x, by: pltpu.roll(x, (by if y_low else -by) % 8, 0)


def from_corner(y_low):
    sub = lax.broadcasted_iota(jnp.int32, (8, 256), 0)
    return 7 - sub if y_low else sub


def pack_k(k, y_low):
    near, turn = from_corner(y_low), turns(y_low)
    return [
        jnp.where(near < 6, k[0], turn(k[4], 2)),
        jnp.where(near < 5, k[1], turn(k[3], 3)),
        jnp.where(near < 4, k[2], turn(k[5], 4)),
    ]


def unpack_k(tiles, y_low):
    turn = turns(y_low)
    one, two, three = tiles
    return [one, two, three, turn(two, -3), turn(one, -2), turn(three, -4)]


def pack_r(r, y_low):
    near, turn = from_corner(y_low), turns(y_low)
    return [
        jnp.where(near < 5, r[0], turn(r[2], 3)),
        jnp.where(near < 4, r[1], jnp.where(near >= 6, turn(r[3], 2), turn(r[4], 4))),
    ]


def unpack_r(tiles, y_low):
    turn = turns(y_low)
    one, two = tiles
    return [one, two, turn(one, -3), turn(two, -2), turn(two, -4)]


def kernel(nw, nn, r_in, k_in, out, *refs):
    (K0, R0, EA, EB, WX, WY, WZ, DG, IV, XS, CK, CKR, CR, CRR, T0, OUT,
     K1, R1, A1, B1, WX1, WY1, WZ1, DG1, IV1, E1S, E1G, T1,
     SB2, G2, KS, GK, K2X, K2S, K3S, K3G, R3S, R3G, F3,
     X3, Y3, Z3, D3, S3, Q3, P3, A3, MB, E2G, E3, DS,
     load, halo_s, halo_r, tail_s, tail_r, kz_s, kz_r, rz_s, rz_r, kx_s, kx_r, e1_s, e1_r,
     k3_s, k3_r, k4_s, k4_r, r3_s, r3_r, e2_s, e2_r, k5_s, k5_r) = refs
    w, n = lax.axis_index("wide"), lax.axis_index("narrow")
    wide = lambda d: lax.rem(w + (d + nw), nw)
    narrow = lambda d: lax.rem(n + (d + nn), nn)

    ny = nw // 8
    in_row, in_column = lax.rem(w, 8), w // 8

    def outside(dx, dy):
        over = jnp.int32(0)
        if dx:
            over = over + jnp.where(w == (nw - 1 if dx > 0 else 0), 1, 0)
            if abs(dx) == 2:
                over = over + jnp.where(w == (nw - 2 if dx > 0 else 1), 1, 0)
        if dy:
            over = over + jnp.where(n == (nn - 1 if dy > 0 else 0), 1, 0)
        return jnp.where(over > 0, 1, 0)

    def remote(src, dst, send, recv, to):
        return pltpu.make_async_remote_copy(
            src_ref=src, dst_ref=dst, send_sem=send, recv_sem=recv, device_id=to, device_id_type=MESH
        )

    load_k = pltpu.make_async_copy(k_in, K0.at[OWN : OWN + 8, 0:16], load.at[0])
    load_r = pltpu.make_async_copy(r_in, R0.at[OWN : OWN + 8, 0:16], load.at[1])
    load_k.start()
    load_r.start()
    barrier = pltpu.get_barrier_semaphore()

    def greet(to):
        pl.semaphore_signal(barrier, inc=1, device_id=to, device_id_type=MESH)

    for dx in (-1, 1):
        for dy in (-1, 1):
            greet((wide(dx), narrow(dy)))
    ring_z, ring_y = far_first(nn), far_first(ny)
    for d in ring_z:
        greet((w, narrow(d)))
    for dx in (-1, 1):
        greet((wide(dx), n))
        greet((wide(2 * dx), n))
    for d in ring_y:
        greet((wide(8 * d), n))
    for d in range(1, 8):
        greet((8 * in_column + lax.rem(in_row + d, 8), n))
    greeted = 4 + len(ring_z) + 4 + len(ring_y) + 7

    zero_planes = jnp.zeros((8, 16, 256), F32)
    K0[PLANES : PLANES + 8, 0:16] = zero_planes
    R0[PLANES : PLANES + 8, 0:16] = zero_planes
    zero_rows = jnp.zeros((16, 256), F32)
    for p in (0, 21):
        K0[p, 16:32] = zero_rows
    for p in (1, 20):
        R0[p, 16:32] = zero_rows
    SB2[1] = jnp.zeros((4, 128), F32)
    K2X[1] = jnp.zeros((32, 128), F32)
    MB[1] = jnp.zeros((2, 32, 128), F32)
    E1S[1] = jnp.zeros((4, 3, 8, 128), F32)
    E3[...] = jnp.zeros((4, 8, 16, 128), F32)
    load_k.wait()
    load_r.wait()

    corners = [(dx, dy) for dx in (-1, 1) for dy in (-1, 1)]
    for i, (dx, dy) in enumerate(corners):
        rows = pl.ds(8, 8) if dy > 0 else pl.ds(0, 8)
        at = lambda a: OWN + (8 - a if dx > 0 else a - 1)
        keep = jnp.where(outside(dx, dy) == 0, 1.0, 0.0).astype(F32)
        for t, tile in enumerate(pack_k([K0[at(a), rows] for a in range(1, 7)], dy > 0)):
            CK[i, t] = tile * keep
        for t, tile in enumerate(pack_r([R0[at(a), rows] for a in range(1, 6)], dy > 0)):
            CR[i, t] = tile * keep

    fine, coarse = iotas(512, 128)
    to_quarter = zero_one(((fine // 256) == (coarse // 64)) & ((fine % 256) // 4 == coarse % 64))
    parts = [
        (K0[OWN + 4 * p, 0:16] + K0[OWN + 4 * p + 1, 0:16]) + (K0[OWN + 4 * p + 2, 0:16] + K0[OWN + 4 * p + 3, 0:16])
        for p in (0, 1)
    ]
    T0[0:16] = times_right(jnp.concatenate(parts, axis=1), to_quarter)
    quarter = (T0[pl.ds(0, 4, stride=4)] + T0[pl.ds(1, 4, stride=4)]) + (
        T0[pl.ds(2, 4, stride=4)] + T0[pl.ds(3, 4, stride=4)]
    )
    KS[...] = quarter * (1.0 / 64.0)

    pl.semaphore_wait(barrier, greeted)

    def send_halo(ref, width, packed, landing, send, recv):
        copies = []

        def push(src, dst, to):
            i = len(copies)
            copies.append(remote(src, dst, send.at[i], recv.at[i], to))
            copies[-1].start()

        for dy in (-1, 1):
            start = jnp.where(outside(0, dy) == 1, PLANES, OWN)
            rows = slice(8, 16) if dy > 0 else slice(0, 8)
            land = slice(24, 32) if dy > 0 else slice(16, 24)
            push(ref.at[pl.ds(start, 8), rows], ref.at[OWN : OWN + 8, land], (w, narrow(dy)))
        for dx in (-1, 1):
            start = OWN + 8 - width if dx > 0 else OWN
            land = OWN - width if dx > 0 else OWN + 8
            start = jnp.where(outside(dx, 0) == 1, PLANES, start)
            push(ref.at[pl.ds(start, width), 0:16], ref.at[land : land + width, 0:16], (wide(dx), n))
        for i, (dx, dy) in enumerate(corners):
            push(packed.at[i], landing.at[3 - i], (wide(dx), narrow(dy)))
        return copies

    def place_corners(ref, landing, unpack, count):
        for i, (dx, dy) in enumerate(corners):
            tiles = unpack([landing[i, t] for t in range(count)], dy < 0)
            rows = pl.ds(24, 8) if dy < 0 else pl.ds(16, 8)
            for a, tile in enumerate(tiles, 1):
                ref[OWN - a if dx < 0 else OWN + 7 + a, rows] = tile

    for d in far_first(nn):
        remote(KS, GK.at[n], kz_s.at[0], kz_r.at[0], (w, narrow(d))).start()
    GK[n] = KS[...]

    halo = send_halo(K0, HALO_K, CK, CKR, halo_s, halo_r)
    tail = send_halo(R0, HALO_R, CR, CRR, tail_s, tail_r)

    remote(GK.at[0 : nn - 1], GK.at[0 : nn - 1], kz_s.at[0], kz_r.at[0], (w, n)).wait_recv()
    for i in range(nn):
        K2X[0, 4 * i : 4 * i + 4] = GK[i]
    slab_k = K2X[0]
    beside = (-2, -1, 1, 2)
    kx = []
    for i, dx in enumerate(beside):
        copy = remote(K2X.at[outside(dx, 0)], K2S.at[2 - dx], kx_s.at[i], kx_r.at[i], (wide(dx), n))
        copy.start()
        kx.append(copy)
    K2S[2] = slab_k

    row, lane = iotas(32, 128)
    own_chunk = (row // 8) == (lane // 32)
    fine, coarse = iotas(128, 128)
    fold = zero_one((fine % 64) // 2 == coarse % 32)
    unfold = zero_one((coarse % 64) // 2 == fine % 32)

    def to_level3(x):
        spread = jnp.where(own_chunk, times_right(x, fold), 0.0)
        T1[...] = (spread[0:8] + spread[8:16]) + (spread[16:24] + spread[24:32])
        return T1[pl.ds(0, 4, stride=2)] + T1[pl.ds(1, 4, stride=2)]

    K3S[...] = 0.125 * to_level3(slab_k)

    for d in far_first(ny):
        remote(K3S, K3G.at[in_row, in_column], k3_s.at[0], k3_r.at[0], (wide(8 * d), n)).start()
    K3G[in_row, in_column] = K3S[...]

    for copy in halo:
        copy.wait_recv()
    place_corners(K0, CKR, unpack_k, 3)
    WX[0] = 0.5 * (K0[0] + K0[1])
    loop(1, 21, weights(K0, WX, WY, WZ, DG, IV), BY_WEIGHTS)

    halve = halve_z()
    k_pairs = jnp.concatenate([K0[2 * q + 1] + K0[2 * q + 2] for q in range(PLANES1)], axis=0)
    T0[...] = times_right(k_pairs, halve)
    K1[...] = (0.125 * (T0[pl.ds(0, 160, stride=2)] + T0[pl.ds(1, 160, stride=2)])).reshape(PLANES1, 16, 128)
    level1 = (WX1, WY1, WZ1)
    set_weights1 = weights(K1, WX1, WY1, WZ1, DG1, IV1)
    WX1[0] = 0.5 * (K1[0] + K1[1])
    loop(1, 9, set_weights1, 8)

    for x1 in range(4):
        E1S[0, x1, 2] = K1[OWN1 + x1, 0:8]
    around = [(dx, dy) for dx in (-1, 0, 1) for dy in (-1, 0, 1) if dx or dy]
    ahead = []
    for i, (dx, dy) in enumerate(corners):
        at = around.index((dx, dy))
        planes = slice(1, 4) if dx > 0 else slice(0, 3)
        src, dst = E1S.at[outside(dx, dy)].at[planes, 2:3], E1G.at[7 - at].at[planes, 2:3]
        ahead.append(remote(src, dst, k5_s.at[i], k5_r.at[i], (wide(dx), narrow(dy))))
        ahead[-1].start()

    for copy in tail:
        copy.wait_recv()
    place_corners(R0, CRR, unpack_r, 2)

    level0 = (WX, WY, WZ)

    def first0(p):
        EA[p] = IV[p] * R0[p]

    loop(1, 21, first0, BY_FIRST)

    def sweep0(source, target):
        def plane(p):
            target[p] = (1.0 - OMEGA) * source[p] + IV[p] * (R0[p] + pull_at(p, source, *level0))

        return plane

    loop(2, 20, sweep0(EA, EB), BY_SWEEP)

    def residual0(i):
        p = 2 * i + 3
        one, two = ((R0[q] - DG[q] * EB[q]) + pull_at(q, EB, *level0) for q in (p, p + 1))
        XS[i] = one + two

    loop(0, 8, residual0, BY_RESIDUAL)
    column = K3G.at[0, 0 : ny - 1]
    remote(column, column, k3_s.at[0], k3_r.at[0], (w, n)).wait_recv()

    def along_row(d, carry):
        to = 8 * in_column + lax.rem(in_row + d, 8)
        remote(K3G.at[in_row], K3G.at[in_row], k4_s.at[0], k4_r.at[0], (to, n)).start()
        return carry

    lax.fori_loop(1, 8, along_row, 0)

    T0[0:256] = times_right(XS[...].reshape(256, 256), halve)
    R1[1:9] = (0.5 * (T0[pl.ds(0, 128, stride=2)] + T0[pl.ds(1, 128, stride=2)])).reshape(8, 16, 128)
    def sweep1(source, target):
        def plane(q):
            target[q] = (1.0 - OMEGA) * source[q] + IV1[q] * (R1[q] + pull_at(q, source, *level1))

        return plane

    for q in range(1, 9):
        A1[q] = IV1[q] * R1[q]
    loop(2, 8, sweep1(A1, B1), 8)
    left = [(R1[q] - DG1[q] * B1[q]) + pull_at(q, B1, *level1) for q in range(OWN1, OWN1 + 4)]
    fine, coarse = iotas(256, 128)
    halve_pair = zero_one(((fine // 128) == (coarse // 64)) & ((fine % 128) // 2 == coarse % 64))
    pair = jnp.concatenate([(left[0] + left[1])[0:8], (left[2] + left[3])[0:8]], axis=1)
    pair = jnp.concatenate([pair, pair], axis=0)
    T0[0:16] = times_right(pair, halve_pair)
    SB2[0] = 0.5 * (T0[pl.ds(0, 4, stride=2)] + T0[pl.ds(1, 4, stride=2)])

    for copy in kx:
        copy.wait_recv()
    for d in far_first(nn) + [0]:
        for dx in (-1, 1, 0) if d else (-1, 1):
            src = SB2.at[outside(dx, 0)]
            remote(src, G2.at[(1 - dx) * nn + n], rz_s.at[0], rz_r.at[0], (wide(dx), narrow(d))).start()
    G2[nn + n] = SB2[0]

    for x1 in range(4):
        E1S[0, x1, 0] = B1[OWN1 + x1, 0:8]
        E1S[0, x1, 1] = R1[OWN1 + x1, 0:8]
    near = []
    for i, (dx, dy) in enumerate(around):
        src, dst = E1S.at[outside(dx, dy)], E1G.at[7 - i]
        planes = slice(1, 4) if dx > 0 else (slice(0, 3) if dx < 0 else slice(0, 4))
        arrays = slice(0, 2) if dx and dy else slice(0, 1)
        src, dst = src.at[planes, arrays], dst.at[planes, arrays]
        copy = remote(src, dst, e1_s.at[i], e1_r.at[i], (wide(dx), narrow(dy)))
        copy.start()
        near.append(copy)

    def to_all(src, dst, send, recv):
        def one(to):
            remote(src, dst.at[w], send.at[0], recv.at[0], (to, n)).start()

        def column_of(y, d):
            return 8 * lax.rem(in_column + y, ny) + lax.rem(in_row + d, 8)

        for y in far_first(ny):
            for d in (4, 5, 3, 2, 6, 7, 1, 0):
                one(column_of(y, d))
        for d in (4, 5, 3, 2, 6, 7, 1):
            one(column_of(0, d))
        dst[w] = src[...]

    def from_all(dst, send, recv):
        return remote(dst.at[0 : nw - 1], dst.at[0 : nw - 1], send.at[0], recv.at[0], (w, n))

    k2 = K2S[...]
    row = lax.broadcasted_iota(jnp.int32, (5, 32, 128), 1)
    cell = lax.broadcasted_iota(jnp.int32, (5, 32, 128), 2)
    odd = cell >= 64
    cell = cell % 64
    none = jnp.zeros((1, 32, 128), F32)

    def above(v):
        turned = pltpu.roll(v, 64, 2)
        after = jnp.concatenate([turned[1:], none], axis=0)
        return jnp.where(odd[: v.shape[0]], after, turned)

    def below(v):
        turned = pltpu.roll(v, 64, 2)
        before = jnp.concatenate([none, turned[:-1]], axis=0)
        return jnp.where(odd[: v.shape[0]], turned, before)

    wx2 = 0.5 * (k2 + above(k2))
    wy2 = jnp.where(row == 31, 0.0, 0.5 * (k2 + pltpu.roll(k2, 31, 1)))
    wz2 = jnp.where(cell == 63, 0.0, 0.5 * (k2 + pltpu.roll(k2, 127, 2)))
    diag2 = (wx2 + below(wx2)) + (wy2 + pltpu.roll(wy2, 1, 1)) + (wz2 + pltpu.roll(wz2, 1, 2))
    diag2 += jnp.where((row == 0) | (row == 31), 0.5 * k2, 0.0) + jnp.where((cell == 0) | (cell == 63), 0.5 * k2, 0.0)
    inv2 = jnp.where(k2 > 0.0, OMEGA / diag2, 0.0)

    def image2(v, at):
        x, y, z = wx2[at], wy2[at], wz2[at]
        total = x * above(v) + below(x * v)
        total += y * pltpu.roll(v, 31, 1) + pltpu.roll(y * v, 1, 1)
        total += z * pltpu.roll(v, 127, 2) + pltpu.roll(z * v, 1, 2)
        return diag2[at] * v - total

    some = slice(1, 4)
    arrived = G2.at[0 : 3 * nn - 1]
    remote(arrived, arrived, rz_s.at[0], rz_r.at[0], (w, n)).wait_recv()
    r2 = jnp.concatenate(
        [jnp.concatenate([G2[b * nn + i] for i in range(nn)], axis=0)[None] for b in range(3)], axis=0
    )
    e2 = inv2[some] * r2
    e2 = e2 + inv2[some] * (r2 - image2(e2, some))
    left2 = (r2 - image2(e2, some))[1]
    R3S[...] = 0.5 * to_level3(left2)
    remote(K3G.at[0:7], K3G.at[0:7], k4_s.at[0], k4_r.at[0], (w, n)).wait_recv()
    to_all(R3S, R3G, r3_s, r3_r)

    MB[0, 0] = e2[1]
    MB[0, 1] = r2[1]
    e2x = []
    for i, dx in enumerate(beside):
        copy = remote(MB.at[outside(dx, 0)], E2G.at[2 - dx], e2_s.at[i], e2_r.at[i], (wide(dx), n))
        copy.start()
        e2x.append(copy)
    E2G[2] = MB[0]

    for copy in ahead + near:
        copy.wait_recv()
    sub = lax.broadcasted_iota(jnp.int32, (8, 128), 0)

    def rim1(x1, which):
        dx = -1 if x1 < 0 else (1 if x1 > 3 else 0)
        after, before = around.index((dx, 1)), around.index((dx, -1))
        return jnp.where(sub < 4, E1G[after, x1 - 4 * dx, which], E1G[before, x1 - 4 * dx, which])

    for x1 in (-3, -2, -1, 4, 5, 6):
        K1[OWN1 + x1, 8:16] = rim1(x1, 2)
        if -2 <= x1 <= 5:
            R1[OWN1 + x1, 8:16] = rim1(x1, 1)
    WX1[0] = 0.5 * (K1[0] + K1[1])
    loop(1, 9, set_weights1, 8)

    def in_order(gathered, target):
        for i in range(nw):
            F3[4 * i : 4 * i + 4] = gathered(i)
        for j in range(4):
            for t in range(8):
                target[j, t] = F3[pl.ds(4 * t + j, 8, stride=32)]

    def next_x(v):
        return jnp.concatenate([v[1:], pltpu.roll(v[0], 7, 0)[None]], axis=0)

    def last_x(v):
        return jnp.concatenate([pltpu.roll(v[7], 1, 0)[None], v[:7]], axis=0)

    in_order(lambda i: K3G[i % 8, i // 8], P3)
    cube = (8, 8, 128)
    tile, row, lane = (lax.broadcasted_iota(jnp.int32, cube, d) for d in range(3))
    first_x, final_x = (tile == 0) & (row == 0), (tile == 7) & (row == 7)
    last_chunk, first_chunk = lane >= 96, lane < 32
    for j in range(4):
        here = P3[j]
        X3[j] = jnp.where(final_x, 0.0, 0.5 * (here + next_x(here)))
        Z3[j] = jnp.where(lane % 32 == 31, 0.0, 0.5 * (here + pltpu.roll(here, 127, 2)))
        if j < 3:
            Y3[j] = 0.5 * (here + P3[j + 1])
        else:
            Y3[j] = jnp.where(last_chunk, 0.0, 0.5 * (here + pltpu.roll(P3[0], 96, 2)))
    for j in range(4):
        here = P3[j]
        lower = Y3[j - 1] if j else pltpu.roll(Y3[3], 32, 2)
        d = (X3[j] + last_x(X3[j])) + (Y3[j] + lower) + (Z3[j] + pltpu.roll(Z3[j], 1, 2))
        rim = jnp.where(first_x | final_x, 0.5, 0.0)
        rim += jnp.where((lane % 32 == 0) | (lane % 32 == 31), 0.5, 0.0)
        if j == 0:
            rim += jnp.where(first_chunk, 0.5, 0.0)
        if j == 3:
            rim += jnp.where(last_chunk, 0.5, 0.0)
        D3[j] = d + rim * here

    from_all(R3G, r3_s, r3_r).wait_recv()
    in_order(lambda i: R3G[i], Q3)

    def total_of(v):
        return jnp.sum(v.reshape(64, 128), keepdims=True).reshape(1, 1, 1)

    def image3(v):
        images = []
        carried = pltpu.roll(Y3[3] * v[3], 32, 2)
        for j in range(4):
            x, y, z = X3[j], Y3[j], Z3[j]
            total = x * next_x(v[j]) + last_x(x * v[j])
            total += z * pltpu.roll(v[j], 127, 2) + pltpu.roll(z * v[j], 1, 2)
            total += y * (v[j + 1] if j < 3 else pltpu.roll(v[0], 96, 2)) + carried
            carried = y * v[j]
            images.append(D3[j] * v[j] - total)
        return images

    norm = alpha = None
    for step in range(COARSE_ITERS):
        images = image3(Q3)
        one, two = jnp.zeros(cube, F32), jnp.zeros(cube, F32)
        for j in range(4):
            rest = Q3[j]
            one += rest * rest
            two += rest * images[j]
        following, pull = total_of(one), total_of(two)
        if step:
            beta = following / norm
            alpha = following / (pull - beta * (following / alpha))
        else:
            alpha = following / pull
        norm = following
        for j in range(4):
            direction = Q3[j] + beta * P3[j] if step else Q3[j]
            result = S3[j] + alpha * direction if step else alpha * direction
            if step == COARSE_ITERS - 1:
                E3[j, :, 1:9] = result
                continue
            carried = images[j] + beta * A3[j] if step else images[j]
            P3[j], A3[j], S3[j] = direction, carried, result
            Q3[j] = Q3[j] - alpha * carried

    for i in range(5):
        x = w + (6 + i)
        for j in range(4):
            value = E3[j, lax.rem(x, 8), pl.ds(x // 8, 1)]
            DS[8 * i + 2 * j : 8 * i + 2 * j + 2] = jnp.broadcast_to(value, (2, 128))
    chunk = lax.broadcasted_iota(jnp.int32, (8, 128), 1) // 32
    rows = [jnp.where(chunk == c, DS[8 * i : 8 * i + 8], 0.0) for i in range(5) for c in range(4)]
    added = times_right(jnp.concatenate(rows, axis=0), unfold).reshape(5, 32, 128)
    for copy in e2x:
        copy.wait_recv()
    r2 = E2G[:, 1]
    e2 = E2G[:, 0] + added
    every = slice(0, 5)
    e2 = e2 + inv2 * (r2 - image2(e2, every))
    e2 = e2 + inv2 * (r2 - image2(e2, every))

    coarse, fine = iotas(128, 256)
    double_pair = zero_one(((fine // 128) == (coarse // 64)) & ((fine % 128) // 2 == coarse % 64))
    stretched = times_right(e2[1:4].reshape(96, 128), double_pair)
    i, y2 = iotas(16, 32)
    y1 = 8 * n + jnp.where(i < 12, i, i - 16)
    pick = zero_one((y1 == 2 * y2) | (y1 == 2 * y2 + 1))
    for b in range(3):
        grown = times_left(pick, stretched[32 * b : 32 * b + 32])
        for p in range(2):
            x2 = 2 * (b - 1) + p
            for x1 in (2 * x2, 2 * x2 + 1):
                if -3 <= x1 <= 6:
                    dx = -1 if x1 < 0 else (1 if x1 > 3 else 0)
                    mine = E1G[around.index((dx, 0)), x1 - 4 * dx, 0] if dx else B1[OWN1 + x1, 0:8]
                    rim = rim1(x1, 0)
                    A1[OWN1 + x1, 0:8] = mine + grown[0:8, 128 * p : 128 * p + 128]
                    A1[OWN1 + x1, 8:16] = rim + grown[8:16, 128 * p : 128 * p + 128]
    loop(1, 9, sweep1(A1, B1), 8)
    loop(2, 8, sweep1(B1, A1), 8)

    stretched = times_right(A1[2:8].reshape(96, 128), double_z())
    i, j = iotas(32, 16)
    twice = zero_one(i // 2 == j)
    for q in range(6):
        grown = times_left(twice, stretched[16 * q : 16 * q + 16])
        for p in (5 + 2 * q, 6 + 2 * q):
            EA[p] = EB[p] + grown
    loop(6, 16, sweep0(EA, EB), BY_SWEEP)

    def last(p):
        here = EB[p, 0:16]
        out[p - OWN] = (1.0 - OMEGA) * here + IV[p, 0:16] * (R0[p, 0:16] + pull_at(p, EB, *level0, keep=16))

    done = []
    for i, first in enumerate((OWN, OWN + 4)):
        loop(first, first + 4, last, BY_LAST)

    for copy in halo + tail + ahead + near + kx + e2x:
        copy.wait_send()
    remote(GK.at[0 : nn - 1], GK.at[0 : nn - 1], kz_s.at[0], kz_r.at[0], (w, n)).wait_send()
    remote(arrived, arrived, rz_s.at[0], rz_r.at[0], (w, n)).wait_send()
    remote(column, column, k3_s.at[0], k3_r.at[0], (w, n)).wait_send()
    remote(K3G.at[0:7], K3G.at[0:7], k4_s.at[0], k4_r.at[0], (w, n)).wait_send()
    from_all(R3G, r3_s, r3_r).wait_send()
    for copy in done:
        copy.wait()


def solution(mesh):
    nw, nn = mesh.shape["wide"], mesh.shape["narrow"]

    def per_device(right_side, coefficient):
        fine = pltpu.VMEM((PLANES, 32, 256), F32)
        with_zeros = pltpu.VMEM((PLANES + 8, 32, 256), F32)
        middle = pltpu.VMEM((PLANES1, 16, 128), F32)
        coarse = pltpu.VMEM((4, 8, 8, 128), F32)
        vmem = lambda *shape: pltpu.VMEM(shape, F32)
        dma = lambda count: pltpu.SemaphoreType.DMA((count,))
        scratch = [with_zeros, with_zeros] + [fine] * 7
        scratch += [vmem(8, 32, 256), vmem(4, 3, 8, 256), vmem(4, 3, 8, 256), vmem(4, 2, 8, 256), vmem(4, 2, 8, 256)]
        scratch += [vmem(320, 128), vmem(8, 16, 256)]
        scratch += [middle] * 9 + [vmem(2, 4, 3, 8, 128), vmem(8, 4, 3, 8, 128), vmem(8, 128)]
        scratch += [vmem(2, 4, 128), vmem(3 * nn, 4, 128), vmem(4, 128), vmem(nn, 4, 128)]
        scratch += [vmem(2, 32, 128), vmem(5, 32, 128)]
        scratch += [vmem(4, 128), vmem(8, nw // 8, 4, 128), vmem(4, 128), vmem(nw, 4, 128), vmem(4 * nw, 128)]
        scratch += [coarse] * 8
        scratch += [vmem(2, 2, 32, 128), vmem(5, 2, 32, 128), vmem(4, 8, 16, 128), vmem(40, 128)]
        scratch += [dma(2), dma(8), dma(8), dma(8), dma(8), dma(1), dma(1), dma(1), dma(1), dma(4), dma(4), dma(8), dma(8)]
        scratch += [dma(1), dma(1), dma(1), dma(1), dma(1), dma(1), dma(4), dma(4), dma(4), dma(4)]
        return pl.pallas_call(
            functools.partial(kernel, nw, nn),
            out_shape=jax.ShapeDtypeStruct((8, 16, 256), F32),
            in_specs=[pl.BlockSpec(memory_space=pltpu.HBM)] * 2,
            out_specs=pl.BlockSpec(memory_space=pltpu.VMEM),
            scratch_shapes=scratch,
            compiler_params=pltpu.CompilerParams(
                collective_id=0, has_side_effects=True, vmem_limit_bytes=55040 * 1024
            ),
        )(right_side, coefficient)

    placed = P("wide", "narrow")
    return jax.shard_map(per_device, mesh=mesh, in_specs=(placed, placed), out_specs=placed, check_vma=False)
```
